128 devices in a mesh: ft: 8 (over y_lo, z), tp: 16 (over y_hi, x, core).
Axes of the slice: x: 4, y: 4 (y_hi: 2, y_lo: 2; y = y_hi * 2 + y_lo), z: 4, core: 2. Of those that a mesh axis runs over, the one named last changes fastest.
Arguments:
- token_rows: int32 [8, 512], P('ft'), may hold values from 0 to 1023
- gate_cache: bfloat16 [8, 1024, 14336], P('ft', None, 'tp'), may hold values from -6 to 6
- up_cache: bfloat16 [8, 1024, 14336], P('ft', None, 'tp'), may hold values from -6 to 6
- down_weight: bfloat16 [8, 14336, 8192], P('ft', 'tp'), may hold values from -3 to 3
- targets: bfloat16 [8, 512, 8192], P('ft'), may hold values from -6 to 6
Outputs:
- merged: float32 [14336, 8192], P('tp', 'ft')
The draws below stay inside these ranges and needn't reach their ends.
Inputs may be any that keep to these rules, and one draw needn't show every extreme that they name: `token_rows`: each id is a row of that fine-adjust's cache.
All inputs are finite; a program needn't handle non-finite values.
Results may differ from the reference program's by a relative error of at most 0.024.
Values may be sent and summed in bfloat16 or wider, within the bound.
No kernel may reach another device: no remote copies, remote signals or barrier semaphores. Data moves between devices by JAX's collectives and lax.ppermute only.
A program may use at most 320 MiB of HBM per device.

```python
import math
import jax
import jax.numpy as jnp
from jax import lax

D = 8192
FF = 14336
TOK = 512
POOL = 1024
FINETUNES = 8


def touch_ends(result, rng, smallest, high):
    shape = result.shape
    index_at = [jax.random.randint(jax.random.fold_in(rng, axis), (), 0, shape[axis]) for axis in range(len(shape))]
    result = result.at[tuple(index_at)].set(smallest)
    longest = shape.index(max(shape))
    index_at[longest] = (index_at[longest] + 1) % shape[longest]
    return result.at[tuple(index_at)].set(high)


def shard_levels(own_key, dims, split, least, largest):
    def one(axis_at, shards_of):
        heights = jax.random.uniform(jax.random.fold_in(jax.random.fold_in(own_key, 6), axis_at), (shards_of,), jnp.float32, least / len(split), largest / len(split))
        return jnp.repeat(jnp.exp(heights), dims[axis_at] // shards_of).reshape((-1,) + (1,) * (len(dims) - axis_at - 1))

    gain = one(*split[0])
    for cut in split[1:]:
        gain = gain * one(*cut)
    return gain


def centred(own_key, dims, spread, limit, shards=(), held_as=jnp.bfloat16):
    entries = spread * jax.random.normal(own_key, dims, jnp.float32)
    if shards:
        entries = entries * shard_levels(own_key, dims, shards, -0.22, 0.18)
    return jnp.clip(entries, -limit, limit).astype(held_as)


def setup_inputs(seed: int = 0) -> dict:
    seeds = jax.random.split(jax.random.key(seed), 6)
    return {
        "token_rows": touch_ends(jax.random.randint(seeds[0], (FINETUNES, TOK), 0, POOL), jax.random.fold_in(seeds[0], 1), 0, POOL - 1).astype(jnp.int32),
        "gate_cache": centred(seeds[1], (FINETUNES, POOL, FF), 1.0, 6.0, ((0, 8), (2, 16))),
        "up_cache": centred(seeds[2], (FINETUNES, POOL, FF), 1.0, 6.0, ((0, 8), (2, 16))),
        "down_weight": centred(seeds[3], (FINETUNES, FF, D), 1.0, 3.0, ((0, 8), (1, 16))),
        "targets": centred(seeds[4], (FINETUNES, TOK, D), 1.0, 6.0, ((0, 8),)),
    }


def reference(token_rows, gate_cache, up_cache, down_weight, targets):
    shrink = 1.0 / math.sqrt(FF)
    numerator = jnp.zeros((FF, D), jnp.float32)
    denominator = jnp.zeros((FF, D), jnp.float32)
    for member in range(FINETUNES):
        picked = token_rows[member]
        gate_rows = jnp.take(gate_cache[member], picked, axis=0).astype(jnp.float32)
        up_rows = jnp.take(up_cache[member], picked, axis=0).astype(jnp.float32)
        hidden = (jax.nn.silu(gate_rows) * up_rows).astype(jnp.bfloat16)
        projection = down_weight[member]
        outputs = jnp.dot(hidden, projection, preferred_element_type=jnp.float32) * shrink
        errors = (outputs - targets[member].astype(jnp.float32)).astype(jnp.bfloat16)
        hidden_wide = hidden.astype(jnp.float32)
        errors_wide = errors.astype(jnp.float32)
        unit_squares = (hidden_wide * hidden_wide).astype(jnp.bfloat16)
        error_squares = (errors_wide * errors_wide).astype(jnp.bfloat16)
        fisher = lax.dot_general(unit_squares, error_squares, (((0,), (0,)), ((), ())), preferred_element_type=jnp.float32) / TOK
        weighted = (fisher * projection.astype(jnp.float32)).astype(jnp.bfloat16)
        fisher_terms = fisher.astype(jnp.bfloat16)
        weighted, fisher_terms = lax.optimization_barrier((weighted, fisher_terms))
        numerator = numerator + weighted.astype(jnp.float32)
        denominator = denominator + fisher_terms.astype(jnp.float32)
    return numerator / (denominator + 1e-06)
```

```python
import math

import jax
import jax.numpy as jnp
from jax import lax
from jax.experimental import pallas as pl
from jax.experimental.pallas import tpu as pltpu
from jax.sharding import PartitionSpec as P

FF = 14336
TOK = 512
POOL = 1024
UNITS = 896
D = 8192
WIDE = 1024
SHRINK = 1.0 / math.sqrt(FF)


def ft_perm(dy, dz):
    return [(i, ((i // 4) ^ dy) * 4 + (i - dz) % 4) for i in range(8)]


def tp_perm(dh, dx, dc):
    out = []
    for i in range(16):
        h, x, c = i // 8, (i // 2) % 4, i % 2
        out.append((i, (h ^ dh) * 8 + ((x - dx) % 4) * 2 + (c ^ dc)))
    return out


def ft_send(value, dy, dz):
    return lax.ppermute(value, "ft", ft_perm(dy, dz))


def tp_send(value, dh, dx, dc):
    return lax.ppermute(value, "tp", tp_perm(dh, dx, dc))


def hidden_kernel(rows_ref, gate_ref, up_ref, hidden_ref, squares_ref):
    rows = rows_ref[...]
    pool = lax.broadcasted_iota(jnp.int32, (TOK, POOL), 1)
    pick = jnp.where(rows == pool, 1.0, 0.0).astype(jnp.bfloat16)
    gate = jnp.dot(pick, gate_ref[...], preferred_element_type=jnp.float32)
    up = jnp.dot(pick, up_ref[...], preferred_element_type=jnp.float32)
    hidden = (gate / (1.0 + jnp.exp(-gate)) * up).astype(jnp.bfloat16)
    hidden_ref[...] = hidden
    wide = hidden.astype(jnp.float32)
    squares_ref[...] = (wide * wide).T.astype(jnp.bfloat16)


def make_hidden(rows, gate, up):
    step = 128
    return pl.pallas_call(
        hidden_kernel,
        grid=(UNITS // step,),
        in_specs=[
            pl.BlockSpec((TOK, 1), lambda i: (0, 0)),
            pl.BlockSpec((POOL, step), lambda i: (0, i)),
            pl.BlockSpec((POOL, step), lambda i: (0, i)),
        ],
        out_specs=[
            pl.BlockSpec((TOK, step), lambda i: (0, i)),
            pl.BlockSpec((step, TOK), lambda i: (i, 0)),
        ],
        out_shape=[
            jax.ShapeDtypeStruct((TOK, UNITS), jnp.bfloat16),
            jax.ShapeDtypeStruct((UNITS, TOK), jnp.bfloat16),
        ],
        compiler_params=pltpu.CompilerParams(vmem_limit_bytes=32 * 2**20),
        cost_estimate=pl.CostEstimate(
            flops=4 * TOK * POOL * UNITS, bytes_accessed=6 * 2**20, transcendentals=TOK * UNITS
        ),
    )(rows, gate, up)


def merge_kernel(n_parts, *refs):
    units = refs[:8]
    weights = refs[8:16]
    parts = refs[16 : 16 + n_parts]
    out_ref = refs[16 + n_parts]
    numerator = None
    for member in range(8):
        squares = jnp.concatenate([part[member] for part in parts], axis=0)
        fisher = jnp.dot(units[member][...], squares, preferred_element_type=jnp.float32) * (1.0 / TOK)
        weighted = (fisher * weights[member][...].astype(jnp.float32)).astype(jnp.bfloat16).astype(jnp.float32)
        term = fisher.astype(jnp.bfloat16).astype(jnp.float32)
        if numerator is None:
            numerator, denominator = weighted, term
        else:
            numerator, denominator = numerator + weighted, denominator + term
    out_ref[...] = numerator / (denominator + 1e-06)


def merge(units, weights, parts):
    step = 256
    tall = 448
    n_parts = len(parts)
    return pl.pallas_call(
        lambda *refs: merge_kernel(n_parts, *refs),
        grid=(UNITS // tall, WIDE // step),
        in_specs=[pl.BlockSpec((tall, TOK), lambda u, i: (u, 0))] * 8
        + [pl.BlockSpec((tall, step), lambda u, i: (u, i))] * 8
        + [pl.BlockSpec((8, TOK // n_parts, step), lambda u, i: (0, 0, i))] * n_parts,
        out_specs=pl.BlockSpec((tall, step), lambda u, i: (u, i)),
        out_shape=jax.ShapeDtypeStruct((UNITS, WIDE), jnp.float32),
        compiler_params=pltpu.CompilerParams(vmem_limit_bytes=48 * 2**20),
        cost_estimate=pl.CostEstimate(
            flops=2 * 8 * TOK * UNITS * WIDE, bytes_accessed=40 * 2**20, transcendentals=0
        ),
    )(*units, *weights, *parts)


def body(token_rows, gate_cache, up_cache, down_weight, targets):
    ft, tp = lax.axis_index("ft"), lax.axis_index("tp")
    y, z = ft // 4, ft % 4
    h, x, core = tp // 8, (tp // 2) % 4, tp % 2
    projection = down_weight[0]

    weights = {}
    for dy, dz in ((1, 0), (0, 2), (1, 2), (0, 1), (0, 3), (1, 1), (1, 3), (0, 0)):
        place = (y ^ dy) * 4 + (z - dz) % 4
        piece = lax.dynamic_slice(projection, (0, place * WIDE), (UNITS, WIDE))
        weights[dy, dz] = ft_send(piece, dy, dz) if (dy, dz) != (0, 0) else piece

    picked = token_rows[0].reshape(2, 4, 2, 32)
    picked = jnp.where(core == 1, picked[::-1], picked)
    picked = lax.dynamic_slice(jnp.concatenate([picked, picked], axis=1), (0, x, 0, 0), (2, 4, 2, 32))
    picked = jnp.where(h == 1, picked[:, :, ::-1], picked).reshape(TOK, 1)
    hidden, squares = make_hidden(picked, gate_cache[0], up_cache[0])

    units = {(0, 0): squares}
    units[1, 0] = ft_send(squares, 1, 0)
    for dz in (1, 3):
        for dy in (0, 1):
            units[dy, dz] = ft_send(units[dy, 0], 0, dz)
    units[0, 2] = ft_send(units[0, 1], 0, 1)
    units[1, 2] = ft_send(units[1, 3], 0, 3)

    def partial(rows):
        return (jnp.dot(rows, projection, preferred_element_type=jnp.float32) * SHRINK).astype(jnp.bfloat16)

    other = tp_send(partial(hidden[256:]), 0, 0, 1)
    own = partial(hidden[:256])
    pair = (own.astype(jnp.float32) + other.astype(jnp.float32)).astype(jnp.bfloat16)
    total = pair[:64].astype(jnp.float32)
    for dx in (1, 2, 3):
        total = total + tp_send(pair[64 * dx : 64 * dx + 64], 0, -dx, 0).astype(jnp.float32)
    far = tp_send(total[32:].astype(jnp.bfloat16), 1, 0, 0)
    outputs = total[:32] + far.astype(jnp.float32)

    first = (core * 8 + x * 2 + h) * 32
    own_targets = lax.dynamic_slice(targets[0], (first, 0), (32, D)).astype(jnp.float32)
    errors = (outputs - own_targets).astype(jnp.bfloat16).astype(jnp.float32)
    error_squares = (errors * errors).astype(jnp.bfloat16)

    order = [(dy, dz) for dy in (0, 1) for dz in (0, 1, 2, 3)]
    pieces = []
    for dy, dz in order:
        place = (y ^ dy) * 4 + (z - dz) % 4
        piece = lax.dynamic_slice(error_squares, (0, place * WIDE), (32, WIDE))
        pieces.append(ft_send(piece, dy, dz) if (dy, dz) != (0, 0) else piece)
    mine = jnp.stack(pieces)
    mine = jnp.concatenate([mine, tp_send(mine, 1, 0, 0)], axis=1)
    row = [mine] + [tp_send(mine, 0, dx, 0) for dx in (1, 2, 3)]
    parts = row + [tp_send(part, 0, 0, 1) for part in row]

    return merge([units[o] for o in order], [weights[o] for o in order], parts)


def solution(mesh):
    placed = (
        P("ft", None),
        P("ft", None, "tp"),
        P("ft", None, "tp"),
        P("ft", "tp", None),
        P("ft", None, None),
    )
    return jax.shard_map(body, mesh=mesh, in_specs=placed, out_specs=P("tp", "ft"), check_vma=False)
```

```python
import math

import jax
import jax.numpy as jnp
from jax import lax
from jax.experimental import pallas as pl
from jax.experimental.pallas import tpu as pltpu
from jax.sharding import Mesh
from jax.sharding import PartitionSpec as P

FF = 14336
TOK = 512
POOL = 1024
UNITS = 896
D = 8192
WIDE = 1024
WP = 768
WQ = WIDE - WP
SHRINK = 1.0 / math.sqrt(FF)
SWAP = [(0, 1), (1, 0)]
BF = jnp.bfloat16
F32 = jnp.float32


def shift(k):
    return [(i, (i + k) % 4) for i in range(4)]


def shape(*dims, dtype=BF):
    return jax.ShapeDtypeStruct(dims, dtype)


def hidden_kernel(place_ref, rows_ref, gate_ref, up_ref, w_ref, hidden_ref, squares_ref, wz0, wz1, wz2, wz3, wy0, wy1, sems):
    y, z = place_ref[0], place_ref[1]
    step = pl.program_id(0)

    def copies():
        out = []
        for dz, piece in enumerate((wz0, wz1, wz2, wz3)):
            for dy in range(2):
                first = ((y + dy) % 2 * 4 + (z + dz) % 4) * WIDE
                out.append((w_ref.at[:, pl.ds(pl.multiple_of(first, 128), WP)], piece.at[dy]))
        for dy, piece in enumerate((wy0, wy1)):
            for dz in range(4):
                first = ((y + dy) % 2 * 4 + (z + dz) % 4) * WIDE + WP
                out.append((w_ref.at[:, pl.ds(pl.multiple_of(first, 128), WQ)], piece.at[dz]))
        return [pltpu.make_async_copy(src, dst, sems.at[i]) for i, (src, dst) in enumerate(out)]

    @pl.when(step == 0)
    def _():
        for copy in copies():
            copy.start()

    pool = lax.broadcasted_iota(jnp.int32, (TOK, POOL), 1)
    pick = jnp.where(rows_ref[...] == pool, 1.0, 0.0).astype(BF)
    gate = jnp.dot(pick, gate_ref[...], preferred_element_type=F32)
    up = jnp.dot(pick, up_ref[...], preferred_element_type=F32)
    hidden = (gate / (1.0 + jnp.exp(-gate)) * up).astype(BF)
    hidden_ref[...] = hidden
    wide = hidden.astype(F32)
    squares_ref[...] = (wide * wide).T.astype(BF)

    @pl.when(step == pl.num_programs(0) - 1)
    def _():
        for copy in copies():
            copy.wait()


def make_hidden(place, rows, gate, up, projection):
    step = 128
    anywhere = pl.BlockSpec(memory_space=pl.ANY)
    return pl.pallas_call(
        hidden_kernel,
        grid_spec=pltpu.PrefetchScalarGridSpec(
            num_scalar_prefetch=1,
            grid=(UNITS // step,),
            in_specs=[
                pl.BlockSpec((TOK, 1), lambda i, s: (0, 0)),
                pl.BlockSpec((POOL, step), lambda i, s: (0, i)),
                pl.BlockSpec((POOL, step), lambda i, s: (0, i)),
                anywhere,
            ],
            out_specs=[
                pl.BlockSpec((TOK, step), lambda i, s: (0, i)),
                pl.BlockSpec((step, TOK), lambda i, s: (i, 0)),
            ]
            + [anywhere] * 6,
            scratch_shapes=[pltpu.SemaphoreType.DMA((16,))],
        ),
        out_shape=[shape(TOK, UNITS), shape(UNITS, TOK)]
        + [shape(2, UNITS, WP)] * 4
        + [shape(4, UNITS, WQ)] * 2,
        compiler_params=pltpu.CompilerParams(vmem_limit_bytes=56 * 2**20),
        cost_estimate=pl.CostEstimate(
            flops=4 * TOK * POOL * UNITS, bytes_accessed=34 * 2**20, transcendentals=TOK * UNITS
        ),
    )(place, rows, gate, up, projection)


def partial_kernel(low, high, hidden_ref, w_ref, own_ref, other_ref):
    product = jnp.dot(hidden_ref[...], w_ref[:, low:high], preferred_element_type=F32) * SHRINK
    own_ref[...] = product[:256].astype(BF)
    other_ref[...] = product[256:].astype(BF)


def partial_outputs(hidden, projection, low, high):
    width = high - low
    return pl.pallas_call(
        lambda *refs: partial_kernel(low, high, *refs),
        grid=(8,),
        in_specs=[
            pl.BlockSpec((TOK, UNITS), lambda j: (0, 0)),
            pl.BlockSpec((UNITS, WIDE), lambda j: (0, j)),
        ],
        out_specs=[pl.BlockSpec((256, width), lambda j: (0, j))] * 2,
        out_shape=[shape(256, 8 * width)] * 2,
        compiler_params=pltpu.CompilerParams(vmem_limit_bytes=40 * 2**20),
        cost_estimate=pl.CostEstimate(
            flops=16 * TOK * UNITS * width, bytes_accessed=24 * 2**20, transcendentals=0
        ),
    )(hidden, projection)


def square_kernel(low, high, place_ref, total_ref, far_ref, targets_ref, out_ref):
    outputs = total_ref[...] + far_ref[...].astype(F32)
    errors = (outputs - targets_ref[:, low:high].astype(F32)).astype(BF).astype(F32)
    out_ref[0] = (errors * errors).astype(BF)


def error_squares(place, total, far, targets, low, high, out_shape, out_index):
    width = high - low
    return pl.pallas_call(
        lambda *refs: square_kernel(low, high, *refs),
        grid_spec=pltpu.PrefetchScalarGridSpec(
            num_scalar_prefetch=1,
            grid=(8,),
            in_specs=[
                pl.BlockSpec((64, width), lambda j, s: (0, j)),
                pl.BlockSpec((64, width), lambda j, s: (0, j)),
                pl.BlockSpec((64, WIDE), lambda j, s: (s[3] * 4 + s[2], j)),
            ],
            out_specs=pl.BlockSpec((1, 64, width), out_index),
        ),
        out_shape=out_shape,
        compiler_params=pltpu.CompilerParams(vmem_limit_bytes=16 * 2**20),
        cost_estimate=pl.CostEstimate(flops=64 * 8 * width * 4, bytes_accessed=4 * 2**20, transcendentals=0),
    )(place, total, far, targets)


def place_tokens(x, parts, scratch, member_of):
    for n, part in enumerate(parts):
        row = n // 4 * 256 + lax.rem(x + 4 - n % 4, 4) * 64
        for k in range(scratch.shape[0]):
            scratch[k, pl.ds(pl.multiple_of(row, 64), 64), :] = part[member_of(k)]


def sums(units, weights, squares, number):
    numerator = denominator = None
    for k in range(number):
        fisher = jnp.dot(units[k], squares(k), preferred_element_type=F32) * (1.0 / TOK)
        weighted = (fisher * weights(k).astype(F32)).astype(BF).astype(F32)
        term = fisher.astype(BF).astype(F32)
        numerator = weighted if numerator is None else numerator + weighted
        denominator = term if denominator is None else denominator + term
    return numerator, denominator


def set_p_kernel(place_ref, *refs):
    units, weights, parts = refs[:4], refs[4:8], refs[8:16]
    out_ref, scratch = refs[16:]
    z, x = place_ref[1], place_ref[2]

    @pl.when(pl.program_id(0) == 0)
    def _():
        place_tokens(x, parts, scratch, lambda k: lax.rem(z + 4 - k, 4))

    numerator, denominator = sums(
        [u[...] for u in units], lambda k: weights[k][0], lambda k: scratch[k], 4
    )
    out_ref[0] = numerator.astype(out_ref.dtype)
    out_ref[1] = denominator.astype(out_ref.dtype)


def set_p(place, units, weights, parts, dy, dtype):
    tall = 224
    return pl.pallas_call(
        set_p_kernel,
        grid_spec=pltpu.PrefetchScalarGridSpec(
            num_scalar_prefetch=1,
            grid=(UNITS // tall,),
            in_specs=[pl.BlockSpec((tall, TOK), lambda u, s: (u, 0))] * 4
            + [pl.BlockSpec((1, tall, WP), lambda u, s: (dy, u, 0))] * 4
            + [pl.BlockSpec((4, 64, WP), lambda u, s: (0, 0, dy))] * 8,
            out_specs=pl.BlockSpec((2, tall, WP), lambda u, s: (0, u, 0)),
            scratch_shapes=[pltpu.VMEM((4, TOK, WP), BF)],
        ),
        out_shape=shape(2, UNITS, WP, dtype=dtype),
        compiler_params=pltpu.CompilerParams(vmem_limit_bytes=40 * 2**20),
        cost_estimate=pl.CostEstimate(
            flops=8 * TOK * UNITS * WP, bytes_accessed=16 * 2**20, transcendentals=0
        ),
    )(place, *units, *weights, *parts)


def set_q_kernel(place_ref, *refs):
    units, weights, parts = refs[:2], refs[2:4], refs[4:12]
    outs, scratch = refs[12:16], refs[16]
    x = place_ref[2]

    @pl.when(pl.program_id(0) == 0)
    def _():
        place_tokens(x, parts, scratch, lambda k: k)

    for dz in (1, 2, 3, 0):
        numerator, denominator = sums(
            [u[...] for u in units],
            lambda k: weights[k][dz],
            lambda k: scratch[k, :, dz * WQ : dz * WQ + WQ],
            2,
        )
        outs[dz][0] = numerator.astype(outs[dz].dtype)
        outs[dz][1] = denominator.astype(outs[dz].dtype)


def set_q(place, units, weights, parts):
    tall = 224
    return pl.pallas_call(
        set_q_kernel,
        grid_spec=pltpu.PrefetchScalarGridSpec(
            num_scalar_prefetch=1,
            grid=(UNITS // tall,),
            in_specs=[pl.BlockSpec((tall, TOK), lambda u, s: (u, 0))] * 2
            + [pl.BlockSpec((4, tall, WQ), lambda u, s: (0, u, 0))] * 2
            + [pl.BlockSpec((2, 64, 4 * WQ), lambda u, s: (0, 0, 0))] * 8,
            out_specs=[pl.BlockSpec((2, tall, WQ), lambda u, s: (0, u, 0))] * 4,
            scratch_shapes=[pltpu.VMEM((2, TOK, 4 * WQ), BF)],
        ),
        out_shape=[shape(2, UNITS, WQ, dtype=F32)] + [shape(2, UNITS, WQ)] * 3,
        compiler_params=pltpu.CompilerParams(vmem_limit_bytes=40 * 2**20),
        cost_estimate=pl.CostEstimate(
            flops=16 * TOK * UNITS * WQ, bytes_accessed=16 * 2**20, transcendentals=0
        ),
    )(place, *units, *weights, *parts)


def quotient_kernel(p_own, p_far, q_own, q_one, q_two, q_three, out_ref):
    def wide(ref, i):
        return ref[i].astype(F32)

    out_ref[:, :WP] = (p_own[0] + wide(p_far, 0)) / (p_own[1] + wide(p_far, 1) + 1e-06)
    numerator = q_own[0] + wide(q_one, 0) + wide(q_two, 0) + wide(q_three, 0)
    denominator = q_own[1] + wide(q_one, 1) + wide(q_two, 1) + wide(q_three, 1)
    out_ref[:, WP:] = numerator / (denominator + 1e-06)


def quotient(p_own, p_far, q_own, q_far):
    tall = 128
    return pl.pallas_call(
        quotient_kernel,
        grid=(UNITS // tall,),
        in_specs=[pl.BlockSpec((2, tall, WP), lambda u: (0, u, 0))] * 2
        + [pl.BlockSpec((2, tall, WQ), lambda u: (0, u, 0))] * 4,
        out_specs=pl.BlockSpec((tall, WIDE), lambda u: (u, 0)),
        out_shape=shape(UNITS, WIDE, dtype=F32),
        compiler_params=pltpu.CompilerParams(vmem_limit_bytes=32 * 2**20),
        cost_estimate=pl.CostEstimate(flops=UNITS * WIDE * 6, bytes_accessed=16 * 2**20, transcendentals=0),
    )(p_own, p_far, q_own, *q_far)


def body(token_rows, gate_cache, up_cache, down_weight, targets):
    y, z, x, core = (lax.axis_index(name) for name in ("y_lo", "z", "x", "core"))
    place = jnp.stack([y, z, x, core]).astype(jnp.int32)
    projection = down_weight[0]

    picked = token_rows[0].reshape(2, TOK // 2)
    picked = jnp.where(core == 1, picked[::-1], picked).reshape(TOK, 1)
    hidden, squares, wz0, wz1, wz2, wz3, wy0, wy1 = make_hidden(
        place, picked, gate_cache[0], up_cache[0], projection
    )
    wz = [wz0] + [lax.ppermute(w, "z", shift(k + 1)) for k, w in enumerate((wz1, wz2, wz3))]
    wy = [wy0, lax.ppermute(wy1, "y_lo", SWAP)]
    uz = [squares] + [lax.ppermute(squares, "z", shift(k)) for k in (1, 2, 3)]
    uy = [squares, lax.ppermute(squares, "y_lo", SWAP)]

    def reduced(low, high):
        own, other = partial_outputs(hidden, projection, low, high)
        pair = (own.astype(F32) + lax.ppermute(other, "core", SWAP).astype(F32)).astype(BF)
        blocks = lax.all_to_all(pair.reshape(4, 64, -1), "x", 0, 0, tiled=True)
        return jnp.sum(blocks.astype(F32), axis=0)

    def far(total):
        return lax.ppermute(total.astype(BF), "y_hi", SWAP)

    def all_tokens(part):
        row = [part] + [lax.ppermute(part, "x", shift(k)) for k in (1, 2, 3)]
        return row + [lax.ppermute(r, "core", SWAP) for r in row]

    total_p = reduced(0, WP)
    far_p = far(total_p)
    total_q = reduced(WP, WIDE)
    far_q = far(total_q)
    squares_p = error_squares(
        place, total_p, far_p, targets[0], 0, WP, shape(4, 64, 2 * WP),
        lambda j, s: (lax.rem(j, 4), 0, lax.rem(j // 4 + s[0], 2)),
    )
    squares_q = error_squares(
        place, total_q, far_q, targets[0], WP, WIDE, shape(2, 64, 4 * WQ),
        lambda j, s: (lax.rem(j // 4 + s[0], 2), 0, lax.rem(lax.rem(j, 4) + 4 - s[1], 4)),
    )
    parts_p = all_tokens(lax.all_to_all(squares_p, "z", 0, 0, tiled=True))
    parts_q = all_tokens(jnp.stack([squares_q[0], lax.ppermute(squares_q[1], "y_lo", SWAP)]))

    p_send = set_p(place, uz, wz, parts_p, 1, BF)
    p_far = lax.ppermute(p_send, "y_lo", SWAP)
    q_own, *q_send = set_q(place, uy, wy, parts_q)
    q_far = [lax.ppermute(q, "z", shift(k + 1)) for k, q in enumerate(q_send)]
    p_own = set_p(place, uz, wz, parts_p, 0, F32)
    return quotient(p_own, p_far, q_own, q_far)


def solution(mesh):
    cut = Mesh(mesh.devices.reshape(2, 4, 2, 4, 2), ("y_lo", "z", "y_hi", "x", "core"))
    ft, tp = ("y_lo", "z"), ("y_hi", "x", "core")
    placed = (P(ft, None), P(ft, None, tp), P(ft, None, tp), P(ft, tp, None), P(ft, None, None))
    return jax.shard_map(body, mesh=cut, in_specs=placed, out_specs=P(tp, ft), check_vma=False)
```

```python
import math

import jax
import jax.numpy as jnp
from jax import lax
from jax.experimental import pallas as pl
from jax.experimental.pallas import tpu as pltpu
from jax.sharding import Mesh
from jax.sharding import PartitionSpec as P

FF = 14336
TOK = 512
POOL = 1024
UNITS = 896
D = 8192
WIDE = 1024
WP = 768
WQ = WIDE - WP
VMEM = 56 * 2**20
SHRINK = 1.0 / math.sqrt(FF)
SWAP = [(0, 1), (1, 0)]
BF = jnp.bfloat16
F32 = jnp.float32
SMALL = pl.CostEstimate(flops=1, bytes_accessed=1, transcendentals=0)


def shift(k):
    return [(i, (i + k) % 4) for i in range(4)]


def shape(*dims, dtype=BF):
    return jax.ShapeDtypeStruct(dims, dtype)


def hidden_kernel(rows_ref, gate_ref, up_ref, hidden_ref, squares_ref):
    pool = lax.broadcasted_iota(jnp.int32, (TOK, POOL), 1)
    pick = jnp.where(rows_ref[...] == pool, 1.0, 0.0).astype(BF)
    gate = jnp.dot(pick, gate_ref[...], preferred_element_type=F32)
    up = jnp.dot(pick, up_ref[...], preferred_element_type=F32)
    hidden = (gate / (1.0 + jnp.exp(-gate)) * up).astype(BF)
    hidden_ref[...] = hidden
    wide = hidden.astype(F32)
    squares_ref[...] = (wide * wide).T.astype(BF)


def make_hidden(rows, gate, up):
    step = 128
    return pl.pallas_call(
        hidden_kernel,
        grid=(UNITS // step,),
        in_specs=[
            pl.BlockSpec((TOK, 1), lambda i: (0, 0)),
            pl.BlockSpec((POOL, step), lambda i: (0, i)),
            pl.BlockSpec((POOL, step), lambda i: (0, i)),
        ],
        out_specs=[
            pl.BlockSpec((TOK, step), lambda i: (0, i)),
            pl.BlockSpec((step, TOK), lambda i: (i, 0)),
        ],
        out_shape=[shape(TOK, UNITS), shape(UNITS, TOK)],
        compiler_params=pltpu.CompilerParams(vmem_limit_bytes=VMEM),
        cost_estimate=SMALL,
    )(rows, gate, up)


def cut_kernel(place_ref, squares_ref, *refs):
    near, far = refs[:3], refs[3:7]
    side, one, three, far_2, near_2 = refs[7:]
    squares = squares_ref[...]
    for out, dz in ((one, 1), (three, 3)):
        out[:, :WP] = far[dz][:, :WP]
        out[:, WP : 2 * WP] = near[dz - 1][:, :WP]
        out[:, 2 * WP :] = squares
    far_2[...] = far[2][:, :WP]
    near_2[...] = near[1][:, :WP]
    for dz in range(4):
        side[:, dz * WQ : dz * WQ + WQ] = far[dz][:, WP:]
    side[:, 4 * WQ :] = squares


def cut(place, squares, projection):
    step = 128

    def columns(dy, dz):
        return pl.BlockSpec((step, WIDE), lambda i, s: (i, lax.rem(s[0] + dy, 2) * 4 + lax.rem(s[1] + dz, 4)))

    def rows_of(width):
        return pl.BlockSpec((step, width), lambda i, s: (i, 0))

    widths = [4 * WQ + TOK, 2 * WP + TOK, 2 * WP + TOK, WP, WP]
    return pl.pallas_call(
        cut_kernel,
        grid_spec=pltpu.PrefetchScalarGridSpec(
            num_scalar_prefetch=1,
            grid=(UNITS // step,),
            in_specs=[rows_of(TOK)]
            + [columns(0, dz) for dz in (1, 2, 3)]
            + [columns(1, dz) for dz in (0, 1, 2, 3)],
            out_specs=[rows_of(width) for width in widths],
        ),
        out_shape=[shape(UNITS, width) for width in widths],
        compiler_params=pltpu.CompilerParams(vmem_limit_bytes=VMEM),
        cost_estimate=SMALL,
    )(place, squares, *[projection] * 7)


def partial_kernel(hidden_ref, w_low, w_high, own_p, other_p, own_q, other_q):
    hidden = hidden_ref[...]
    low = (jnp.dot(hidden, w_low[...], preferred_element_type=F32) * SHRINK).astype(BF)
    high = (jnp.dot(hidden, w_high[...], preferred_element_type=F32) * SHRINK).astype(BF)
    edge = WP - WIDE // 2
    for ref_p, ref_q, rows in ((own_p, own_q, slice(0, 256)), (other_p, other_q, slice(256, 512))):
        ref_p[:, : WIDE // 2] = low[rows]
        ref_p[:, WIDE // 2 :] = high[rows, :edge]
        ref_q[...] = high[rows, edge:]


def partial_outputs(hidden, projection):
    half = WIDE // 2
    return pl.pallas_call(
        partial_kernel,
        grid=(8,),
        in_specs=[
            pl.BlockSpec((TOK, UNITS), lambda j: (0, 0)),
            pl.BlockSpec((UNITS, half), lambda j: (0, 2 * j)),
            pl.BlockSpec((UNITS, half), lambda j: (0, 2 * j + 1)),
        ],
        out_specs=[pl.BlockSpec((256, WP), lambda j: (0, j))] * 2
        + [pl.BlockSpec((256, WQ), lambda j: (0, j))] * 2,
        out_shape=[shape(256, 8 * WP)] * 2 + [shape(256, 8 * WQ)] * 2,
        compiler_params=pltpu.CompilerParams(vmem_limit_bytes=VMEM),
        cost_estimate=SMALL,
    )(hidden, projection, projection)


def square_kernel(low, high, put, place_ref, total_ref, far_ref, targets_ref, out_ref):
    width = high - low
    for j in range(4):
        columns = slice(j * width, j * width + width)
        outputs = total_ref[:, columns] + far_ref[:, columns].astype(F32)
        wanted = targets_ref[:, j * WIDE + low : j * WIDE + high].astype(F32)
        errors = (outputs - wanted).astype(BF).astype(F32)
        put(place_ref, out_ref, j, (errors * errors).astype(BF))


def put_p(place_ref, out_ref, j, value):
    out_ref[j] = value


def put_q(place_ref, out_ref, j, value):
    first = lax.rem(j + 4 - place_ref[1], 4) * WQ
    out_ref[0, :, pl.ds(pl.multiple_of(first, 128), WQ)] = value


def error_squares(place, total, far, targets, low, high, out_shape, out_spec, put):
    width = high - low
    return pl.pallas_call(
        lambda *refs: square_kernel(low, high, put, *refs),
        grid_spec=pltpu.PrefetchScalarGridSpec(
            num_scalar_prefetch=1,
            grid=(2,),
            in_specs=[
                pl.BlockSpec((64, 4 * width), lambda j, s: (0, j)),
                pl.BlockSpec((64, 4 * width), lambda j, s: (0, j)),
                pl.BlockSpec((64, 4 * WIDE), lambda j, s: (s[3] * 4 + s[2], j)),
            ],
            out_specs=out_spec,
        ),
        out_shape=out_shape,
        compiler_params=pltpu.CompilerParams(vmem_limit_bytes=VMEM),
        cost_estimate=SMALL,
    )(place, total, far, targets)


def place_tokens(parts, scratch, member_of):
    for c, part in enumerate(parts):
        for place in range(4):
            row = c * 256 + place * 64
            for k in range(scratch.shape[0]):
                scratch[k, row : row + 64, :] = part[place, member_of(k)]


def sums(units, weights, squares, number):
    numerator = denominator = None
    for k in range(number):
        fisher = jnp.dot(units[k], squares(k), preferred_element_type=F32) * (1.0 / TOK)
        weighted = (fisher * weights(k).astype(F32)).astype(BF).astype(F32)
        term = fisher.astype(BF).astype(F32)
        numerator = weighted if numerator is None else numerator + weighted
        denominator = term if denominator is None else denominator + term
    return numerator, denominator


def set_p_kernel(place_ref, own_units, *refs):
    halves, weights, parts, out_ref, scratch = refs[:6], refs[6:10], refs[10:12], refs[12], refs[13]
    z = place_ref[1]

    @pl.when(pl.program_id(0) == 0)
    def _():
        place_tokens(parts, scratch, lambda k: lax.rem(z + 4 - k, 4))

    units = [own_units[...]]
    units += [jnp.concatenate([halves[2 * k][...], halves[2 * k + 1][...]], axis=1) for k in range(3)]
    numerator, denominator = sums(units, lambda k: weights[k][:, :WP], lambda k: scratch[k], 4)
    out_ref[0] = numerator.astype(out_ref.dtype)
    out_ref[1] = denominator.astype(out_ref.dtype)


def set_p(place, squares, one, u_2, three, weight_2, projection, parts, dy, dtype):
    tall = 224
    half = TOK // 2

    def halves(first):
        return [pl.BlockSpec((tall, half), lambda u, s, i=i: (u, first // half + i)) for i in (0, 1)]

    def columns(i):
        return pl.BlockSpec((tall, WP), lambda u, s: (u, i))

    return pl.pallas_call(
        set_p_kernel,
        grid_spec=pltpu.PrefetchScalarGridSpec(
            num_scalar_prefetch=1,
            grid=(UNITS // tall,),
            in_specs=[pl.BlockSpec((tall, TOK), lambda u, s: (u, 0))]
            + [*halves(2 * WP), *[pl.BlockSpec((tall, half), lambda u, s: (u, 0))] * 2, *halves(2 * WP)]
            + [pl.BlockSpec((tall, WIDE), lambda u, s: (u, lax.rem(s[0] + dy, 2) * 4 + s[1]))]
            + [columns(1 - dy), columns(0), columns(1 - dy)]
            + [pl.BlockSpec((4, 4, 64, WP), lambda u, s: (0, 0, 0, dy))] * 2,
            out_specs=pl.BlockSpec((2, tall, WP), lambda u, s: (0, u, 0)),
            scratch_shapes=[pltpu.VMEM((4, TOK, WP), BF)],
        ),
        out_shape=shape(2, UNITS, WP, dtype=dtype),
        compiler_params=pltpu.CompilerParams(vmem_limit_bytes=VMEM),
        cost_estimate=SMALL,
    )(place, squares, one, one, *u_2, three, three, projection, one, weight_2, three, *parts)


def set_q_kernel(place_ref, own_units, far_units, own_0, own_1, own_2, own_3, far_weights, *refs):
    own_weights = (own_0, own_1, own_2, own_3)
    parts, outs, scratch = refs[:2], refs[2:6], refs[6]

    @pl.when(pl.program_id(0) == 0)
    def _():
        place_tokens(parts, scratch, lambda k: k)

    for dz in (1, 2, 3, 0):
        columns = slice(dz * WQ, dz * WQ + WQ)
        weights = (own_weights[dz][:, WP:], far_weights[:, columns])
        numerator, denominator = sums(
            [own_units[...], far_units[...]], lambda k: weights[k], lambda k: scratch[k, :, columns], 2
        )
        outs[dz][0] = numerator.astype(outs[dz].dtype)
        outs[dz][1] = denominator.astype(outs[dz].dtype)


def set_q(place, units, projection, far, parts):
    tall = 224

    def own(dz):
        return pl.BlockSpec((tall, WIDE), lambda u, s: (u, s[0] * 4 + lax.rem(s[1] + dz, 4)))

    return pl.pallas_call(
        set_q_kernel,
        grid_spec=pltpu.PrefetchScalarGridSpec(
            num_scalar_prefetch=1,
            grid=(UNITS // tall,),
            in_specs=[
                pl.BlockSpec((tall, TOK), lambda u, s: (u, 0)),
                pl.BlockSpec((tall, TOK), lambda u, s: (u, 4 * WQ // TOK)),
            ]
            + [own(dz) for dz in range(4)]
            + [pl.BlockSpec((tall, 4 * WQ), lambda u, s: (u, 0))]
            + [pl.BlockSpec((4, 2, 64, 4 * WQ), lambda u, s: (0, 0, 0, 0))] * 2,
            out_specs=[pl.BlockSpec((2, tall, WQ), lambda u, s: (0, u, 0))] * 4,
            scratch_shapes=[pltpu.VMEM((2, TOK, 4 * WQ), BF)],
        ),
        out_shape=[shape(2, UNITS, WQ, dtype=F32)] + [shape(2, UNITS, WQ)] * 3,
        compiler_params=pltpu.CompilerParams(vmem_limit_bytes=VMEM),
        cost_estimate=SMALL,
    )(place, units, far, projection, projection, projection, projection, far, *parts)


def quotient_kernel(p_own, p_far, q_own, q_one, q_two, q_three, out_ref):
    def wide(ref, i):
        return ref[i].astype(F32)

    out_ref[:, :WP] = (p_own[0] + wide(p_far, 0)) / (p_own[1] + wide(p_far, 1) + 1e-06)
    numerator = q_own[0] + wide(q_one, 0) + wide(q_two, 0) + wide(q_three, 0)
    denominator = q_own[1] + wide(q_one, 1) + wide(q_two, 1) + wide(q_three, 1)
    out_ref[:, WP:] = numerator / (denominator + 1e-06)


def quotient(p_own, p_far, q_own, q_far):
    tall = 128
    return pl.pallas_call(
        quotient_kernel,
        grid=(UNITS // tall,),
        in_specs=[pl.BlockSpec((2, tall, WP), lambda u: (0, u, 0))] * 2
        + [pl.BlockSpec((2, tall, WQ), lambda u: (0, u, 0))] * 4,
        out_specs=pl.BlockSpec((tall, WIDE), lambda u: (u, 0)),
        out_shape=shape(UNITS, WIDE, dtype=F32),
        compiler_params=pltpu.CompilerParams(vmem_limit_bytes=VMEM),
        cost_estimate=SMALL,
    )(p_own, p_far, q_own, *q_far)


def body(token_rows, gate_cache, up_cache, down_weight, targets):
    y, z, x, core = (lax.axis_index(name) for name in ("y_lo", "z", "x", "core"))
    place = jnp.stack([y, z, x, core]).astype(jnp.int32)
    projection = down_weight[0]

    def send(value, axis, k=1):
        return lax.ppermute(value, axis, shift(k) if axis in ("z", "x") else SWAP)

    together = lax.optimization_barrier

    picked = token_rows[0].reshape(2, TOK // 2)
    picked = jnp.where(core == 1, picked[::-1], picked).reshape(TOK, 1)
    hidden, squares = make_hidden(picked, gate_cache[0], up_cache[0])

    own_p, other_p, own_q, other_q = partial_outputs(hidden, projection)
    other_p, squares = together((other_p, squares))
    side, one, three, far_2, near_2 = cut(place, squares, projection)
    one, three, side = send(one, "z", 1), send(three, "z", 3), send(side, "y_lo")

    def pair(own, other):
        both = (own.astype(F32) + send(other, "core").astype(F32)).astype(BF)
        return both.reshape(4, 64, -1)

    def over_x(blocks):
        return lax.all_to_all(blocks, "x", 0, 0, tiled=True)

    def total(blocks):
        return jnp.sum(blocks.astype(F32), axis=0)

    def gathered(part):
        return over_x(jnp.broadcast_to(part[None], (4,) + part.shape))

    blocks_p = over_x(pair(own_p, other_p))
    pair_q = pair(own_q, other_q)
    blocks_p, pair_q = together((blocks_p, pair_q))
    total_p = total(blocks_p)
    half_p, side = together((total_p.astype(BF), side))
    far_p = send(half_p, "y_hi")
    total_q = total(over_x(pair_q))
    squares_p = error_squares(
        place, total_p, far_p, targets[0], 0, WP, shape(4, 64, 2 * WP),
        pl.BlockSpec((4, 64, WP), lambda j, s: (0, 0, lax.rem(j + s[0], 2))), put_p,
    )
    squares_p, one, three, total_q = together((squares_p, one, three, total_q))
    far_q = send(total_q.astype(BF), "y_hi")
    mine_p = lax.all_to_all(squares_p, "z", 0, 0, tiled=True)
    middle = 2 * WP + TOK // 2
    u_2 = (one[:, 2 * WP : middle], three[:, middle:])
    mine_p, far_q, far_2, u_2 = together((mine_p, far_q, far_2, u_2))

    u_2 = (send(u_2[0], "z", 1), send(u_2[1], "z", 3))
    far_2 = send(far_2, "z", 2)
    row_p = gathered(mine_p)
    squares_q = error_squares(
        place, total_q, far_q, targets[0], WP, WIDE, shape(2, 64, 4 * WQ),
        pl.BlockSpec((1, 64, 4 * WQ), lambda j, s: (lax.rem(j + s[0], 2), 0, 0)), put_q,
    )
    mine_q = jnp.stack([squares_q[0], send(squares_q[1], "y_lo")])
    row_p, far_2, u_2, mine_q, near_2 = together((row_p, far_2, u_2, mine_q, near_2))

    near_2 = send(near_2, "z", 2)
    parts_p = [row_p, send(row_p, "core")]
    p_far = send(set_p(place, squares, one, u_2, three, far_2, projection, parts_p, 1, BF), "y_lo")
    row_q = gathered(mine_q)
    parts_q = [row_q, send(row_q, "core")]
    q_sums = set_q(place, squares, projection, side, parts_q)
    q_sums, near_2 = together((q_sums, near_2))
    q_own, *q_send = q_sums
    q_far = [send(q, "z", k + 1) for k, q in enumerate(q_send)]
    p_own = set_p(place, squares, one, u_2, three, near_2, projection, parts_p, 0, F32)
    return quotient(p_own, p_far, q_own, q_far)


def solution(mesh):
    cut = Mesh(mesh.devices.reshape(2, 4, 2, 4, 2), ("y_lo", "z", "y_hi", "x", "core"))
    ft, tp = ("y_lo", "z"), ("y_hi", "x", "core")
    placed = (P(ft, None), P(ft, None, tp), P(ft, None, tp), P(ft, tp, None), P(ft, None, None))
    return jax.shard_map(body, mesh=cut, in_specs=placed, out_specs=P(tp, ft), check_vma=False)
```

```python
import math

import jax
import jax.numpy as jnp
from jax import lax
from jax.experimental import pallas as pl
from jax.experimental.pallas import tpu as pltpu
from jax.sharding import Mesh
from jax.sharding import PartitionSpec as P

FF = 14336
TOK = 512
POOL = 1024
UNITS = 896
D = 8192
WIDE = 1024
WP = 768
WQ = WIDE - WP
WN = 640
VMEM = 56 * 2**20
SHRINK = 1.0 / math.sqrt(FF)
SWAP = [(0, 1), (1, 0)]
BF = jnp.bfloat16
F32 = jnp.float32
SMALL = pl.CostEstimate(flops=1, bytes_accessed=1, transcendentals=0)


def shift(k):
    return [(i, (i + k) % 4) for i in range(4)]


def shape(*dims, dtype=BF):
    return jax.ShapeDtypeStruct(dims, dtype)


def hidden_kernel(place_ref, rows_ref, gate_ref, up_ref, hidden_ref, squares_ref, pick):
    @pl.when(pl.program_id(0) == 0)
    def _():
        rows = rows_ref[...]
        other = jnp.concatenate([rows[:, TOK // 2 :], rows[:, : TOK // 2]], axis=1)
        rows = jnp.where(place_ref[3] == 1, other, rows)
        pool = lax.broadcasted_iota(jnp.int32, (POOL, TOK), 0)
        pick[...] = jnp.where(rows == pool, 1.0, 0.0).astype(BF)

    def picked(ref):
        return lax.dot_general(ref[...], pick[...], (((0,), (0,)), ((), ())), preferred_element_type=F32)

    gate, up = picked(gate_ref), picked(up_ref)
    hidden = (gate / (1.0 + jnp.exp(-gate)) * up).astype(BF)
    wide = hidden.astype(F32)
    hidden_ref[...] = wide.T.astype(BF)
    squares_ref[...] = (wide * wide).astype(BF)


def make_hidden(place, rows, gate, up):
    step = 128
    return pl.pallas_call(
        hidden_kernel,
        grid_spec=pltpu.PrefetchScalarGridSpec(
            num_scalar_prefetch=1,
            grid=(UNITS // step,),
            in_specs=[
                pl.BlockSpec((1, TOK), lambda i, s: (0, 0)),
                pl.BlockSpec((POOL, step), lambda i, s: (0, i)),
                pl.BlockSpec((POOL, step), lambda i, s: (0, i)),
            ],
            out_specs=[
                pl.BlockSpec((TOK, step), lambda i, s: (0, i)),
                pl.BlockSpec((step, TOK), lambda i, s: (i, 0)),
            ],
            scratch_shapes=[pltpu.VMEM((POOL, TOK), BF)],
        ),
        out_shape=[shape(TOK, UNITS), shape(UNITS, TOK)],
        compiler_params=pltpu.CompilerParams(vmem_limit_bytes=VMEM),
        cost_estimate=SMALL,
    )(place, rows, gate, up)


def cut_first_kernel(place_ref, squares_ref, near_1, near_3, far_0, far_1, far_2, far_3, side, one, three):
    squares = squares_ref[...]
    for out, far, near in ((one, far_1, near_1), (three, far_3, near_3)):
        out[:, :WP] = far[:, :WP]
        out[:, WP : 2 * WP] = near[:, :WP]
        out[:, 2 * WP :] = squares
    for dz, far in enumerate((far_0, far_1, far_2, far_3)):
        side[:, dz * WQ : dz * WQ + WQ] = far[:, WP:]


def cut_second_kernel(place_ref, near, far, near_low, near_high, far_two):
    near_low[...] = near[:, :WN]
    near_high[...] = near[:, WN:WP]
    far_two[...] = far[:, :WP]


def cut(kernel, place, extra, projection, places, widths):
    step = 128

    def columns(dy, dz):
        return pl.BlockSpec((step, WIDE), lambda i, s: (i, lax.rem(s[0] + dy, 2) * 4 + lax.rem(s[1] + dz, 4)))

    def rows_of(width):
        return pl.BlockSpec((step, width), lambda i, s: (i, 0))

    return pl.pallas_call(
        kernel,
        grid_spec=pltpu.PrefetchScalarGridSpec(
            num_scalar_prefetch=1,
            grid=(UNITS // step,),
            in_specs=[rows_of(TOK)] * len(extra) + [columns(dy, dz) for dy, dz in places],
            out_specs=[rows_of(width) for width in widths],
        ),
        out_shape=[shape(UNITS, width) for width in widths],
        compiler_params=pltpu.CompilerParams(vmem_limit_bytes=VMEM),
        cost_estimate=SMALL,
    )(place, *extra, *[projection] * len(places))


def partial_kernel(hidden_ref, w_low, w_high, own_p, other_p, own_q, other_q):
    hidden = hidden_ref[...]
    low = (jnp.dot(hidden, w_low[...], preferred_element_type=F32) * SHRINK).astype(BF)
    high = (jnp.dot(hidden, w_high[...], preferred_element_type=F32) * SHRINK).astype(BF)
    edge = WP - WIDE // 2
    for ref_p, ref_q, rows in ((own_p, own_q, slice(0, 256)), (other_p, other_q, slice(256, 512))):
        ref_p[:, : WIDE // 2] = low[rows]
        ref_p[:, WIDE // 2 :] = high[rows, :edge]
        ref_q[...] = high[rows, edge:]


def partial_outputs(hidden, projection):
    half = WIDE // 2
    return pl.pallas_call(
        partial_kernel,
        grid=(8,),
        in_specs=[
            pl.BlockSpec((TOK, UNITS), lambda j: (0, 0)),
            pl.BlockSpec((UNITS, half), lambda j: (0, 2 * j)),
            pl.BlockSpec((UNITS, half), lambda j: (0, 2 * j + 1)),
        ],
        out_specs=[pl.BlockSpec((256, WP), lambda j: (0, j))] * 2
        + [pl.BlockSpec((256, WQ), lambda j: (0, j))] * 2,
        out_shape=[shape(256, 8 * WP)] * 2 + [shape(256, 8 * WQ)] * 2,
        compiler_params=pltpu.CompilerParams(vmem_limit_bytes=VMEM),
        cost_estimate=SMALL,
    )(hidden, projection, projection)


def square_kernel(low, high, put, place_ref, total_ref, far_ref, targets_ref, *outs):
    width = high - low
    for k in range(4):
        place = lax.rem(place_ref[1] + k, 4)
        columns = pl.ds(pl.multiple_of(place * width, 128), width)
        outputs = total_ref[:, columns].astype(F32) + far_ref[:, columns].astype(F32)
        wanted = targets_ref[:, pl.ds(pl.multiple_of(place * WIDE + low, 128), width)].astype(F32)
        errors = (outputs - wanted).astype(BF).astype(F32)
        put(outs, k, (errors * errors).astype(BF))


def put_p(outs, k, value):
    outs[k][...] = value


def put_q(outs, k, value):
    outs[0][0, :, k * WQ : k * WQ + WQ] = value


def error_squares(place, total, far, targets, low, high, out_shape, out_spec, put):
    width = high - low
    return pl.pallas_call(
        lambda *refs: square_kernel(low, high, put, *refs),
        grid_spec=pltpu.PrefetchScalarGridSpec(
            num_scalar_prefetch=1,
            grid=(2,),
            in_specs=[
                pl.BlockSpec((64, 4 * width), lambda j, s: (0, j)),
                pl.BlockSpec((64, 4 * width), lambda j, s: (0, j)),
                pl.BlockSpec((64, 4 * WIDE), lambda j, s: (s[3] * 4 + s[2], j)),
            ],
            out_specs=out_spec,
        ),
        out_shape=out_shape,
        compiler_params=pltpu.CompilerParams(vmem_limit_bytes=VMEM),
        cost_estimate=SMALL,
    )(place, total, far, targets)


def place_tokens(parts, scratch):
    for c, part in enumerate(parts):
        for place in range(4):
            row = c * 256 + place * 64
            for k in range(scratch.shape[0]):
                scratch[k, row : row + 64, :] = part[place, k]


def sums(units, weights, squares, number):
    numerator = denominator = None
    for k in range(number):
        fisher = jnp.dot(units[k], squares(k), preferred_element_type=F32) * (1.0 / TOK)
        weighted = (fisher * weights(k).astype(F32)).astype(BF).astype(F32)
        term = fisher.astype(BF).astype(F32)
        numerator = weighted if numerator is None else numerator + weighted
        denominator = term if denominator is None else denominator + term
    return numerator, denominator


def set_p_kernel(n_two, place_ref, own_units, *refs):
    halves, own, one, two, three = refs[:6], refs[6], refs[7], refs[8 : 8 + n_two], refs[8 + n_two]
    parts, (out_ref, scratch) = refs[9 + n_two : 11 + n_two], refs[11 + n_two :]

    @pl.when(pl.program_id(0) == 0)
    def _():
        place_tokens(parts, scratch)

    def whole(*parts):
        return jnp.concatenate([part[...] for part in parts], axis=1)

    units = [own_units[...]] + [whole(halves[2 * k], halves[2 * k + 1]) for k in range(3)]
    weights = [own[:, :WP], one[...], whole(*two), three[...]]
    numerator, denominator = sums(units, lambda k: weights[k], lambda k: scratch[k], 4)
    out_ref[0] = numerator.astype(out_ref.dtype)
    out_ref[1] = denominator.astype(out_ref.dtype)


def set_p(place, squares, one, u_2, three, two, projection, parts, dy, dtype):
    tall = 224
    half = TOK // 2

    def halves(first):
        return [pl.BlockSpec((tall, half), lambda u, s, i=i: (u, first // half + i)) for i in (0, 1)]

    def columns(i):
        return pl.BlockSpec((tall, WP), lambda u, s: (u, i))

    from_two = [pl.BlockSpec((tall, part.shape[1]), lambda u, s: (u, 0)) for part in two]

    return pl.pallas_call(
        lambda *refs: set_p_kernel(len(two), *refs),
        grid_spec=pltpu.PrefetchScalarGridSpec(
            num_scalar_prefetch=1,
            grid=(UNITS // tall,),
            in_specs=[pl.BlockSpec((tall, TOK), lambda u, s: (u, 0))]
            + [*halves(2 * WP), *[pl.BlockSpec((tall, half), lambda u, s: (u, 0))] * 2, *halves(2 * WP)]
            + [pl.BlockSpec((tall, WIDE), lambda u, s: (u, lax.rem(s[0] + dy, 2) * 4 + s[1]))]
            + [columns(1 - dy), *from_two, columns(1 - dy)]
            + [pl.BlockSpec((4, 4, 64, WP), lambda u, s: (0, 0, 0, dy))] * 2,
            out_specs=pl.BlockSpec((2, tall, WP), lambda u, s: (0, u, 0)),
            scratch_shapes=[pltpu.VMEM((4, TOK, WP), BF)],
        ),
        out_shape=shape(2, UNITS, WP, dtype=dtype),
        compiler_params=pltpu.CompilerParams(vmem_limit_bytes=VMEM),
        cost_estimate=SMALL,
    )(place, squares, one, one, *u_2, three, three, projection, one, *two, three, *parts)


def set_q_kernel(place_ref, own_units, far_units, own_0, own_1, own_2, own_3, far_weights, *refs):
    own_weights = (own_0, own_1, own_2, own_3)
    parts, outs, scratch = refs[:2], refs[2:6], refs[6]

    @pl.when(pl.program_id(0) == 0)
    def _():
        place_tokens(parts, scratch)

    for dz in (1, 2, 3, 0):
        columns = slice(dz * WQ, dz * WQ + WQ)
        weights = (own_weights[dz][:, WP:], far_weights[:, columns])
        numerator, denominator = sums(
            [own_units[...], far_units[...]], lambda k: weights[k], lambda k: scratch[k, :, columns], 2
        )
        outs[dz][0] = numerator.astype(outs[dz].dtype)
        outs[dz][1] = denominator.astype(outs[dz].dtype)


def set_q(place, units, far_units, projection, far, parts):
    tall = 224

    def own(dz):
        return pl.BlockSpec((tall, WIDE), lambda u, s: (u, s[0] * 4 + lax.rem(s[1] + dz, 4)))

    return pl.pallas_call(
        set_q_kernel,
        grid_spec=pltpu.PrefetchScalarGridSpec(
            num_scalar_prefetch=1,
            grid=(UNITS // tall,),
            in_specs=[
                pl.BlockSpec((tall, TOK), lambda u, s: (u, 0)),
                pl.BlockSpec((tall, TOK), lambda u, s: (u, 0)),
            ]
            + [own(dz) for dz in range(4)]
            + [pl.BlockSpec((tall, 4 * WQ), lambda u, s: (u, 0))]
            + [pl.BlockSpec((4, 2, 64, 4 * WQ), lambda u, s: (0, 0, 0, 0))] * 2,
            out_specs=[pl.BlockSpec((2, tall, WQ), lambda u, s: (0, u, 0))] * 4,
            scratch_shapes=[pltpu.VMEM((2, TOK, 4 * WQ), BF)],
        ),
        out_shape=[shape(2, UNITS, WQ, dtype=F32)] + [shape(2, UNITS, WQ)] * 3,
        compiler_params=pltpu.CompilerParams(vmem_limit_bytes=VMEM),
        cost_estimate=SMALL,
    )(place, units, far_units, projection, projection, projection, projection, far, *parts)


def quotient_kernel(columns, *refs):
    out_ref = refs[-1]

    def total(i):
        value = refs[0][i]
        for ref in refs[1 : -1 - (columns.start > 0)]:
            value = value + ref[i].astype(F32)
        return value

    out_ref[...] = total(0) / (total(1) + 1e-06)


def quotient(columns, terms, before=None):
    tall = 224
    width = columns.stop - columns.start
    place = columns.start // width
    given = [] if before is None else [before]
    return pl.pallas_call(
        lambda *refs: quotient_kernel(columns, *refs),
        grid=(UNITS // tall,),
        in_specs=[pl.BlockSpec((2, tall, width), lambda u: (0, u, 0))] * len(terms)
        + [pl.BlockSpec(memory_space=pl.ANY)] * len(given),
        out_specs=pl.BlockSpec((tall, width), lambda u: (u, place)),
        out_shape=shape(UNITS, WIDE, dtype=F32),
        input_output_aliases={len(terms): 0} if given else {},
        compiler_params=pltpu.CompilerParams(vmem_limit_bytes=VMEM),
        cost_estimate=SMALL,
    )(*terms, *given)


def body(token_rows, gate_cache, up_cache, down_weight, targets):
    y, z, x, core = (lax.axis_index(name) for name in ("y_lo", "z", "x", "core"))
    place = jnp.stack([y, z, x, core]).astype(jnp.int32)
    projection = down_weight[0]

    def send(value, axis, k=1):
        return lax.ppermute(value, axis, shift(k) if axis in ("z", "x") else SWAP)

    together = lax.optimization_barrier

    hidden, squares = make_hidden(place, token_rows, gate_cache[0], up_cache[0])

    own_p, other_p, own_q, other_q = partial_outputs(hidden, projection)
    other_p, squares = together((other_p, squares))
    side, one, three = cut(
        cut_first_kernel, place, [squares], projection,
        [(0, 1), (0, 3), (1, 0), (1, 1), (1, 2), (1, 3)], [4 * WQ, 2 * WP + TOK, 2 * WP + TOK],
    )
    one, three, side = send(one, "z", 1), send(three, "z", 3), send(side, "y_lo")

    def pair(own, other):
        both = (own.astype(F32) + send(other, "core").astype(F32)).astype(BF)
        return both.reshape(4, 64, -1)

    def over_x(blocks):
        return lax.all_to_all(blocks, "x", 0, 0, tiled=True)

    def total(blocks):
        return jnp.sum(blocks.astype(F32), axis=0).astype(BF)

    def gathered(part):
        return over_x(jnp.broadcast_to(part[None], (4,) + part.shape))

    blocks_p = over_x(pair(own_p, other_p))
    pair_q = pair(own_q, other_q)
    blocks_p, pair_q = together((blocks_p, pair_q))
    total_p = total(blocks_p)
    total_p, side = together((total_p, side))
    far_p = send(total_p, "y_hi")
    total_q = total(over_x(pair_q))
    squares_p = error_squares(
        place, total_p, far_p, targets[0], 0, WP, [shape(64, 2 * WP)] * 4,
        [pl.BlockSpec((64, WP), lambda j, s: (0, lax.rem(j + s[0], 2)))] * 4, put_p,
    )
    near_low, near_high, far_2 = cut(
        cut_second_kernel, place, [], projection, [(0, 2), (1, 2)], [WN, WP - WN, WP]
    )
    squares_p, one, three, total_q, far_2, near_low, near_high = together(
        (squares_p, one, three, total_q, far_2, near_low, near_high)
    )
    far_q = send(total_q, "y_hi")
    mine_p = jnp.stack([squares_p[0]] + [send(squares_p[k], "z", k) for k in (1, 2, 3)])
    middle = 2 * WP + TOK // 2
    u_2 = (one[:, 2 * WP : middle], three[:, middle:])
    mine_p, far_q, far_2, u_2, squares_late = together((mine_p, far_q, far_2, u_2, squares))

    u_2 = (send(u_2[0], "z", 1), send(u_2[1], "z", 3))
    far_2, u_side = send(far_2, "z", 2), send(squares_late, "y_lo")
    row_p = gathered(mine_p)
    squares_q = error_squares(
        place, total_q, far_q, targets[0], WP, WIDE, shape(2, 64, 4 * WQ),
        pl.BlockSpec((1, 64, 4 * WQ), lambda j, s: (lax.rem(j + s[0], 2), 0, 0)), put_q,
    )
    mine_q = jnp.stack([squares_q[0], send(squares_q[1], "y_lo")])
    row_p, far_2, u_2, u_side, mine_q, near_low, near_high = together(
        (row_p, far_2, u_2, u_side, mine_q, near_low, near_high)
    )

    near_low = send(near_low, "z", 2)
    parts_p = [row_p, send(row_p, "core")]
    p_far = send(set_p(place, squares, one, u_2, three, [far_2], projection, parts_p, 1, BF), "y_lo")
    row_q, near_low, near_high = together((gathered(mine_q), near_low, near_high))
    near_high = send(near_high, "z", 2)
    parts_q = [row_q, send(row_q, "core")]
    q_sums = set_q(place, squares, u_side, projection, side, parts_q)
    q_sums, near_high = together((q_sums, near_high))
    q_own, *q_send = q_sums
    q_far = [send(q, "z", k + 1) for k, q in enumerate(q_send)]
    p_own = set_p(place, squares, one, u_2, three, [near_low, near_high], projection, parts_p, 0, F32)
    merged = quotient(slice(0, WP), [p_own, p_far])
    return quotient(slice(WP, WIDE), [q_own, *q_far], merged)


def solution(mesh):
    cut = Mesh(mesh.devices.reshape(2, 4, 2, 4, 2), ("y_lo", "z", "y_hi", "x", "core"))
    ft, tp = ("y_lo", "z"), ("y_hi", "x", "core")
    placed = (P(ft, None), P(ft, None, tp), P(ft, None, tp), P(ft, tp, None), P(ft, None, None))
    return jax.shard_map(body, mesh=cut, in_specs=placed, out_specs=P(tp, ft), check_vma=False)
```

```python
import math

import jax
import jax.numpy as jnp
from jax import lax
from jax.experimental import pallas as pl
from jax.experimental.pallas import tpu as pltpu
from jax.sharding import Mesh
from jax.sharding import PartitionSpec as P

FF = 14336
TOK = 512
POOL = 1024
UNITS = 896
D = 8192
WIDE = 1024
WP = 768
WQ = WIDE - WP
WN = 640
WN2 = 512
VMEM = 56 * 2**20
SHRINK = 1.0 / math.sqrt(FF)
SWAP = [(0, 1), (1, 0)]
BF = jnp.bfloat16
F32 = jnp.float32
SMALL = pl.CostEstimate(flops=1, bytes_accessed=1, transcendentals=0)


def shift(k):
    return [(i, (i + k) % 4) for i in range(4)]


def shape(*dims, dtype=BF):
    return jax.ShapeDtypeStruct(dims, dtype)


def hidden_kernel(place_ref, rows_ref, gate_ref, up_ref, hidden_ref, squares_ref):
    rows = rows_ref[...]
    other = jnp.concatenate([rows[:, TOK // 2 :], rows[:, : TOK // 2]], axis=1)
    rows = jnp.where(place_ref[3] == 1, other, rows)
    pool = lax.broadcasted_iota(jnp.int32, (POOL, TOK), 0)
    pick = jnp.where(rows == pool, 1.0, 0.0).T.astype(BF)
    gate = jnp.dot(pick, gate_ref[...], preferred_element_type=F32)
    up = jnp.dot(pick, up_ref[...], preferred_element_type=F32)
    hidden = (gate / (1.0 + jnp.exp(-gate)) * up).astype(BF)
    hidden_ref[...] = hidden
    wide = hidden.astype(F32)
    squares_ref[...] = (wide * wide).T.astype(BF)


def make_hidden(place, rows, gate, up):
    return pl.pallas_call(
        hidden_kernel,
        grid_spec=pltpu.PrefetchScalarGridSpec(
            num_scalar_prefetch=1,
            grid=(1,),
            in_specs=[
                pl.BlockSpec((1, TOK), lambda i, s: (0, 0)),
                pl.BlockSpec((POOL, UNITS), lambda i, s: (0, 0)),
                pl.BlockSpec((POOL, UNITS), lambda i, s: (0, 0)),
            ],
            out_specs=[
                pl.BlockSpec((TOK, UNITS), lambda i, s: (0, 0)),
                pl.BlockSpec((UNITS, TOK), lambda i, s: (0, 0)),
            ],
        ),
        out_shape=[shape(TOK, UNITS), shape(UNITS, TOK)],
        compiler_params=pltpu.CompilerParams(vmem_limit_bytes=VMEM),
        cost_estimate=SMALL,
    )(place, rows, gate, up)


def cut_first_kernel(place_ref, squares_ref, near_1, near_3, far_0, far_1, far_2, far_3, side, one, three):
    squares = squares_ref[...]
    for out, far, near in ((one, far_1, near_1), (three, far_3, near_3)):
        out[:, :WP] = far[:, :WP]
        out[:, WP : WP + TOK] = squares
        out[:, WP + TOK :] = near[:, :WN]
    for dz, far in enumerate((far_0, far_1, far_2, far_3)):
        side[:, dz * WQ : dz * WQ + WQ] = far[:, WP:]


def cut_second_kernel(place_ref, near_1, near_2, near_3, far_2, late_1, early_2, late_2, late_3, far_two):
    late_1[...] = near_1[:, WN:WP]
    late_3[...] = near_3[:, WN:WP]
    early_2[...] = near_2[:, :WN2]
    late_2[...] = near_2[:, WN2:WP]
    far_two[...] = far_2[:, :WP]


def cut(kernel, place, extra, projection, places, widths):
    step = 224

    def columns(dy, dz):
        return pl.BlockSpec((step, WIDE), lambda i, s: (i, lax.rem(s[0] + dy, 2) * 4 + lax.rem(s[1] + dz, 4)))

    def rows_of(width):
        return pl.BlockSpec((step, width), lambda i, s: (i, 0))

    return pl.pallas_call(
        kernel,
        grid_spec=pltpu.PrefetchScalarGridSpec(
            num_scalar_prefetch=1,
            grid=(UNITS // step,),
            in_specs=[rows_of(TOK)] * len(extra) + [columns(dy, dz) for dy, dz in places],
            out_specs=[rows_of(width) for width in widths],
        ),
        out_shape=[shape(UNITS, width) for width in widths],
        compiler_params=pltpu.CompilerParams(vmem_limit_bytes=VMEM),
        cost_estimate=SMALL,
    )(place, *extra, *[projection] * len(places))


def partial_kernel(hidden_ref, w_low, w_high, own_p, other_p, own_q, other_q):
    hidden = hidden_ref[...]
    low = (jnp.dot(hidden, w_low[...], preferred_element_type=F32) * SHRINK).astype(BF)
    high = (jnp.dot(hidden, w_high[...], preferred_element_type=F32) * SHRINK).astype(BF)
    edge = WP - WIDE // 2
    for ref_p, ref_q, rows in ((own_p, own_q, slice(0, 256)), (other_p, other_q, slice(256, 512))):
        ref_p[:, : WIDE // 2] = low[rows]
        ref_p[:, WIDE // 2 :] = high[rows, :edge]
        ref_q[...] = high[rows, edge:]


def partial_outputs(hidden, projection):
    half = WIDE // 2
    return pl.pallas_call(
        partial_kernel,
        grid=(8,),
        in_specs=[
            pl.BlockSpec((TOK, UNITS), lambda j: (0, 0)),
            pl.BlockSpec((UNITS, half), lambda j: (0, 2 * j)),
            pl.BlockSpec((UNITS, half), lambda j: (0, 2 * j + 1)),
        ],
        out_specs=[pl.BlockSpec((256, WP), lambda j: (0, j))] * 2
        + [pl.BlockSpec((256, WQ), lambda j: (0, j))] * 2,
        out_shape=[shape(256, 8 * WP)] * 2 + [shape(256, 8 * WQ)] * 2,
        compiler_params=pltpu.CompilerParams(vmem_limit_bytes=VMEM),
        cost_estimate=SMALL,
    )(hidden, projection, projection)


def square_kernel(low, high, put, place_ref, total_ref, far_ref, targets_ref, *outs):
    width = high - low
    for k in range(4):
        place = lax.rem(place_ref[1] + k, 4)
        columns = pl.ds(pl.multiple_of(place * width, 128), width)
        outputs = total_ref[:, columns].astype(F32) + far_ref[:, columns].astype(F32)
        wanted = targets_ref[:, pl.ds(pl.multiple_of(place * WIDE + low, 128), width)].astype(F32)
        errors = (outputs - wanted).astype(BF).astype(F32)
        put(outs, k, (errors * errors).astype(BF))


def put_p(outs, k, value):
    outs[k][...] = value


def put_q(outs, k, value):
    outs[0][0, :, k * WQ : k * WQ + WQ] = value


def error_squares(place, total, far, targets, low, high, out_shape, out_spec, put):
    width = high - low
    return pl.pallas_call(
        lambda *refs: square_kernel(low, high, put, *refs),
        grid_spec=pltpu.PrefetchScalarGridSpec(
            num_scalar_prefetch=1,
            grid=(2,),
            in_specs=[
                pl.BlockSpec((64, 4 * width), lambda j, s: (0, j)),
                pl.BlockSpec((64, 4 * width), lambda j, s: (0, j)),
                pl.BlockSpec((64, 4 * WIDE), lambda j, s: (s[3] * 4 + s[2], j)),
            ],
            out_specs=out_spec,
        ),
        out_shape=out_shape,
        compiler_params=pltpu.CompilerParams(vmem_limit_bytes=VMEM),
        cost_estimate=SMALL,
    )(place, total, far, targets)


def place_tokens(parts, scratch):
    for c, part in enumerate(parts):
        for place in range(4):
            row = c * 256 + place * 64
            for k in range(scratch.shape[0]):
                scratch[k, row : row + 64, :] = part[place, k]


def sums(units, weights, squares, number):
    numerator = denominator = None
    for k in range(number):
        fisher = jnp.dot(units[k], squares(k), preferred_element_type=F32) * (1.0 / TOK)
        weighted = (fisher * weights(k).astype(F32)).astype(BF).astype(F32)
        term = fisher.astype(BF).astype(F32)
        numerator = weighted if numerator is None else numerator + weighted
        denominator = term if denominator is None else denominator + term
    return numerator, denominator


def set_p_kernel(counts, place_ref, own_units, own, *refs):
    refs = list(refs)
    groups = []
    for count in counts:
        groups.append(jnp.concatenate([ref[...] for ref in refs[:count]], axis=1))
        del refs[:count]
    parts, (out_ref, scratch) = refs[:2], refs[2:]

    @pl.when(pl.program_id(0) == 0)
    def _():
        place_tokens(parts, scratch)

    units, weights = [own_units[...]] + groups[:3], [own[:, :WP]] + groups[3:]
    numerator, denominator = sums(units, lambda k: weights[k], lambda k: scratch[k], 4)
    out_ref[0] = numerator.astype(out_ref.dtype)
    out_ref[1] = denominator.astype(out_ref.dtype)


def set_p(place, squares, projection, moved, parts, dy, dtype, first=0, count=4):
    tall = 224
    pieces = [piece for group in moved for piece in group]
    return pl.pallas_call(
        lambda *refs: set_p_kernel([len(group) for group in moved], *refs),
        grid_spec=pltpu.PrefetchScalarGridSpec(
            num_scalar_prefetch=1,
            grid=(count,),
            in_specs=[
                pl.BlockSpec((tall, TOK), lambda u, s: (u + first, 0)),
                pl.BlockSpec((tall, WIDE), lambda u, s: (u + first, lax.rem(s[0] + dy, 2) * 4 + s[1])),
            ]
            + [pl.BlockSpec((tall, width), lambda u, s, i=i: (u + first, i)) for _, width, i in pieces]
            + [pl.BlockSpec((4, 4, 64, WP), lambda u, s: (0, 0, 0, dy))] * 2,
            out_specs=pl.BlockSpec((2, tall, WP), lambda u, s: (0, u, 0)),
            scratch_shapes=[pltpu.VMEM((4, TOK, WP), BF)],
        ),
        out_shape=shape(2, count * tall, WP, dtype=dtype),
        compiler_params=pltpu.CompilerParams(vmem_limit_bytes=VMEM),
        cost_estimate=SMALL,
    )(place, squares, projection, *[array for array, _, _ in pieces], *parts)


def set_q_kernel(place_ref, own_units, far_units, own_0, own_1, own_2, own_3, far_weights, *refs):
    own_weights = (own_0, own_1, own_2, own_3)
    parts, outs, scratch = refs[:2], refs[2:6], refs[6]

    @pl.when(pl.program_id(0) == 0)
    def _():
        place_tokens(parts, scratch)

    for dz in (1, 2, 3, 0):
        columns = slice(dz * WQ, dz * WQ + WQ)
        weights = (own_weights[dz][...], far_weights[:, columns])
        numerator, denominator = sums(
            [own_units[...], far_units[...]], lambda k: weights[k], lambda k: scratch[k, :, columns], 2
        )
        outs[dz][0] = numerator.astype(outs[dz].dtype)
        outs[dz][1] = denominator.astype(outs[dz].dtype)


def set_q(place, units, far_units, projection, far, parts):
    tall = 224

    def own(dz):
        return pl.BlockSpec((tall, WQ), lambda u, s: (u, (s[0] * 4 + lax.rem(s[1] + dz, 4)) * (WIDE // WQ) + WP // WQ))

    return pl.pallas_call(
        set_q_kernel,
        grid_spec=pltpu.PrefetchScalarGridSpec(
            num_scalar_prefetch=1,
            grid=(UNITS // tall,),
            in_specs=[
                pl.BlockSpec((tall, TOK), lambda u, s: (u, 0)),
                pl.BlockSpec((tall, TOK), lambda u, s: (u, 0)),
            ]
            + [own(dz) for dz in range(4)]
            + [pl.BlockSpec((tall, 4 * WQ), lambda u, s: (u, 0))]
            + [pl.BlockSpec((4, 2, 64, 4 * WQ), lambda u, s: (0, 0, 0, 0))] * 2,
            out_specs=[pl.BlockSpec((2, tall, WQ), lambda u, s: (0, u, 0))] * 4,
            scratch_shapes=[pltpu.VMEM((2, TOK, 4 * WQ), BF)],
        ),
        out_shape=[shape(2, UNITS, WQ, dtype=F32)] + [shape(2, UNITS, WQ)] * 3,
        compiler_params=pltpu.CompilerParams(vmem_limit_bytes=VMEM),
        cost_estimate=SMALL,
    )(place, units, far_units, projection, projection, projection, projection, far, *parts)


def quotient_kernel(n_given, *refs):
    out_ref = refs[-1]

    def total(i):
        value = refs[0][i]
        for ref in refs[1 : -1 - n_given]:
            value = value + ref[i].astype(F32)
        return value

    out_ref[...] = total(0) / (total(1) + 1e-06)


def quotient(columns, terms, before=None, first=0, count=4):
    tall = 224
    width = columns.stop - columns.start
    place = columns.start // width
    given = [] if before is None else [before]
    return pl.pallas_call(
        lambda *refs: quotient_kernel(len(given), *refs),
        grid=(count,),
        in_specs=[
            pl.BlockSpec((2, tall, width), lambda u, start=first * (term.shape[1] == UNITS): (0, u + start, 0))
            for term in terms
        ]
        + [pl.BlockSpec(memory_space=pl.ANY)] * len(given),
        out_specs=pl.BlockSpec((tall, width), lambda u: (u + first, place)),
        out_shape=shape(UNITS, WIDE, dtype=F32),
        input_output_aliases={len(terms): 0} if given else {},
        compiler_params=pltpu.CompilerParams(vmem_limit_bytes=VMEM),
        cost_estimate=SMALL,
    )(*terms, *given)


def body(token_rows, gate_cache, up_cache, down_weight, targets):
    y, z, x, core = (lax.axis_index(name) for name in ("y_lo", "z", "x", "core"))
    place = jnp.stack([y, z, x, core]).astype(jnp.int32)
    projection = down_weight[0]

    def send(value, axis, k=1):
        return lax.ppermute(value, axis, shift(k) if axis in ("z", "x") else SWAP)

    together = lax.optimization_barrier

    hidden, squares = make_hidden(place, token_rows, gate_cache[0], up_cache[0])

    own_p, other_p, own_q, other_q = partial_outputs(hidden, projection)
    other_p, squares = together((other_p, squares))
    side, one, three = cut(
        cut_first_kernel, place, [squares], projection,
        [(0, 1), (0, 3), (1, 0), (1, 1), (1, 2), (1, 3)], [4 * WQ, WP + WN + TOK, WP + WN + TOK],
    )
    one, three, side = send(one, "z", 1), send(three, "z", 3), send(side, "y_lo")

    def pair(own, other):
        both = (own.astype(F32) + send(other, "core").astype(F32)).astype(BF)
        return both.reshape(4, 64, -1)

    def over_x(blocks):
        return lax.all_to_all(blocks, "x", 0, 0, tiled=True)

    def total(blocks):
        return jnp.sum(blocks.astype(F32), axis=0).astype(BF)

    def gathered(part):
        return over_x(jnp.broadcast_to(part[None], (4,) + part.shape))

    blocks_p = over_x(pair(own_p, other_p))
    pair_q = pair(own_q, other_q)
    blocks_p, pair_q = together((blocks_p, pair_q))
    total_p = total(blocks_p)
    total_p, side = together((total_p, side))
    far_p = send(total_p, "y_hi")
    total_q = total(over_x(pair_q))
    squares_p = error_squares(
        place, total_p, far_p, targets[0], 0, WP, [shape(64, 2 * WP)] * 4,
        [pl.BlockSpec((64, WP), lambda j, s: (0, lax.rem(j + s[0], 2)))] * 4, put_p,
    )
    late_1, early_2, late_2, late_3, far_2 = cut(
        cut_second_kernel, place, [], projection,
        [(0, 1), (0, 2), (0, 3), (1, 2)], [WP - WN, WN2, WP - WN2, WP - WN, WP],
    )
    squares_p, one, three, total_q, far_2, early_2, late = together(
        (squares_p, one, three, total_q, far_2, early_2, (late_1, late_2, late_3))
    )
    far_q = send(total_q, "y_hi")
    mine_p = jnp.stack([squares_p[0]] + [send(squares_p[k], "z", k) for k in (1, 2, 3)])
    middle = WP + TOK // 2
    u_2 = (one[:, WP:middle], three[:, middle : WP + TOK])
    mine_p, far_q, far_2, u_2, squares_late = together((mine_p, far_q, far_2, u_2, squares))

    u_2 = (send(u_2[0], "z", 1), send(u_2[1], "z", 3))
    far_2, u_side = send(far_2, "z", 2), send(squares_late, "y_lo")
    row_p = gathered(mine_p)
    squares_q = error_squares(
        place, total_q, far_q, targets[0], WP, WIDE, shape(2, 64, 4 * WQ),
        pl.BlockSpec((1, 64, 4 * WQ), lambda j, s: (lax.rem(j + s[0], 2), 0, 0)), put_q,
    )
    mine_q = jnp.stack([squares_q[0], send(squares_q[1], "y_lo")])
    row_p, far_2, u_2, u_side, mine_q, early_2, late = together(
        (row_p, far_2, u_2, u_side, mine_q, early_2, late)
    )

    half = TOK // 2

    def units_in(array):
        return [(array, half, WP // half), (array, half, WP // half + 1)]

    def near_in(array, late):
        return [(array, WN, (WP + TOK) // WN), (late, WP - WN, 0)]

    units = [units_in(one), [(u, half, 0) for u in u_2], units_in(three)]
    fars = [[(array, WP, 0)] for array in (one, far_2, three)]
    early_2 = send(early_2, "z", 2)
    parts_p = [row_p, send(row_p, "core")]
    p_far = send(set_p(place, squares, projection, units + fars, parts_p, 1, BF), "y_lo")
    row_q, early_2, late = together((gathered(mine_q), early_2, late))
    late = [send(piece, "z", k + 1) for k, piece in enumerate(late)]
    parts_q = [row_q, send(row_q, "core")]
    q_sums = set_q(place, squares, u_side, projection, side, parts_q)
    q_sums, late = together((q_sums, late))
    q_own, *q_send = q_sums
    q_far = [send(q, "z", k + 1) for k, q in enumerate(q_send)]
    nears = [
        near_in(one, late[0]),
        [(early_2, WN2, 0), (late[1], WP - WN2, 0)],
        near_in(three, late[2]),
    ]
    p_own = set_p(place, squares, projection, units + nears, parts_p, 0, F32)
    merged = quotient(slice(0, WP), [p_own, p_far])
    return quotient(slice(WP, WIDE), [q_own, *q_far], merged)


def solution(mesh):
    cut = Mesh(mesh.devices.reshape(2, 4, 2, 4, 2), ("y_lo", "z", "y_hi", "x", "core"))
    ft, tp = ("y_lo", "z"), ("y_hi", "x", "core")
    placed = (P(ft, None), P(ft, None, tp), P(ft, None, tp), P(ft, tp, None), P(ft, None, None))
    return jax.shard_map(body, mesh=cut, in_specs=placed, out_specs=P(tp, ft), check_vma=False)
```

```python
import math

import jax
import jax.numpy as jnp
from jax import lax
from jax.experimental import pallas as pl
from jax.experimental.pallas import tpu as pltpu
from jax.sharding import Mesh
from jax.sharding import PartitionSpec as P

FF = 14336
TOK = 512
POOL = 1024
UNITS = 896
D = 8192
WIDE = 1024
WP = 768
WQ = WIDE - WP
WN = 640
WN2 = 640
VMEM = 56 * 2**20
SHRINK = 1.0 / math.sqrt(FF)
SWAP = [(0, 1), (1, 0)]
BF = jnp.bfloat16
F32 = jnp.float32
SMALL = pl.CostEstimate(flops=1, bytes_accessed=1, transcendentals=0)


def shift(k):
    return [(i, (i + k) % 4) for i in range(4)]


def shape(*dims, dtype=BF):
    return jax.ShapeDtypeStruct(dims, dtype)


def hidden_kernel(place_ref, rows_ref, gate_ref, up_ref, hidden_ref, squares_ref):
    rows = rows_ref[...]
    other = jnp.concatenate([rows[:, TOK // 2 :], rows[:, : TOK // 2]], axis=1)
    rows = jnp.where(place_ref[3] == 1, other, rows)
    pool = lax.broadcasted_iota(jnp.int32, (POOL, TOK), 0)
    pick = jnp.where(rows == pool, 1.0, 0.0).T.astype(BF)
    gate = jnp.dot(pick, gate_ref[...], preferred_element_type=F32)
    up = jnp.dot(pick, up_ref[...], preferred_element_type=F32)
    hidden = (gate / (1.0 + jnp.exp(-gate)) * up).astype(BF)
    hidden_ref[...] = hidden
    wide = hidden.astype(F32)
    squares_ref[...] = (wide * wide).T.astype(BF)


def make_hidden(place, rows, gate, up):
    return pl.pallas_call(
        hidden_kernel,
        grid_spec=pltpu.PrefetchScalarGridSpec(
            num_scalar_prefetch=1,
            grid=(1,),
            in_specs=[
                pl.BlockSpec((1, TOK), lambda i, s: (0, 0)),
                pl.BlockSpec((POOL, UNITS), lambda i, s: (0, 0)),
                pl.BlockSpec((POOL, UNITS), lambda i, s: (0, 0)),
            ],
            out_specs=[
                pl.BlockSpec((TOK, UNITS), lambda i, s: (0, 0)),
                pl.BlockSpec((UNITS, TOK), lambda i, s: (0, 0)),
            ],
        ),
        out_shape=[shape(TOK, UNITS), shape(UNITS, TOK)],
        compiler_params=pltpu.CompilerParams(vmem_limit_bytes=VMEM),
        cost_estimate=SMALL,
    )(place, rows, gate, up)


def cut_first_kernel(place_ref, squares_ref, near_1, near_3, far_0, far_1, far_2, far_3, side, one, three):
    squares = squares_ref[...]
    for out, far, near in ((one, far_1, near_1), (three, far_3, near_3)):
        out[:, :WP] = far[:, :WP]
        out[:, WP : WP + TOK] = squares
        out[:, WP + TOK :] = near[:, :WN]
    for dz, far in enumerate((far_0, far_1, far_2, far_3)):
        side[:, dz * WQ : dz * WQ + WQ] = far[:, WP:]


def cut_second_kernel(place_ref, near_1, near_2, near_3, far_2, late_1, early_2, late_2, late_3, far_two):
    late_1[...] = near_1[:, WN:WP]
    late_3[...] = near_3[:, WN:WP]
    early_2[...] = near_2[:, :WN2]
    late_2[...] = near_2[:, WN2:WP]
    far_two[...] = far_2[:, :WP]


def cut(kernel, place, extra, projection, places, widths):
    step = 224

    def columns(dy, dz):
        return pl.BlockSpec((step, WIDE), lambda i, s: (i, lax.rem(s[0] + dy, 2) * 4 + lax.rem(s[1] + dz, 4)))

    def rows_of(width):
        return pl.BlockSpec((step, width), lambda i, s: (i, 0))

    return pl.pallas_call(
        kernel,
        grid_spec=pltpu.PrefetchScalarGridSpec(
            num_scalar_prefetch=1,
            grid=(UNITS // step,),
            in_specs=[rows_of(TOK)] * len(extra) + [columns(dy, dz) for dy, dz in places],
            out_specs=[rows_of(width) for width in widths],
        ),
        out_shape=[shape(UNITS, width) for width in widths],
        compiler_params=pltpu.CompilerParams(vmem_limit_bytes=50 * 2**20),
        cost_estimate=SMALL,
    )(place, *extra, *[projection] * len(places))


def partial_kernel(hidden_ref, *refs):
    hidden = hidden_ref[...]
    *streams, own, other = refs
    for i, stream in enumerate(streams):
        columns = slice(i * WQ, i * WQ + WQ)
        product = (jnp.dot(hidden, stream[...], preferred_element_type=F32) * SHRINK).astype(BF)
        own[:, columns] = product[:256]
        other[:, columns] = product[256:]


def partial_outputs(hidden, projection, low, high):
    width = high - low
    streams = [
        pl.BlockSpec((UNITS, WQ), lambda j, i=i: (0, j * (WIDE // WQ) + i)) for i in range(low // WQ, high // WQ)
    ]
    return pl.pallas_call(
        partial_kernel,
        grid=(8,),
        in_specs=[pl.BlockSpec((TOK, UNITS), lambda j: (0, 0)), *streams],
        out_specs=[pl.BlockSpec((256, width), lambda j: (0, j))] * 2,
        out_shape=[shape(256, 8 * width)] * 2,
        compiler_params=pltpu.CompilerParams(vmem_limit_bytes=50 * 2**20),
        cost_estimate=SMALL,
    )(hidden, *[projection] * len(streams))


def square_kernel(low, high, put, place_ref, total_ref, far_ref, targets_ref, *outs):
    width = high - low
    for k in range(4):
        place = lax.rem(place_ref[1] + k, 4)
        columns = pl.ds(pl.multiple_of(place * width, 128), width)
        outputs = total_ref[:, columns].astype(F32) + far_ref[:, columns].astype(F32)
        wanted = targets_ref[:, pl.ds(pl.multiple_of(place * WIDE + low, 128), width)].astype(F32)
        errors = (outputs - wanted).astype(BF).astype(F32)
        put(outs, k, (errors * errors).astype(BF))


def put_p(outs, k, value):
    outs[k][...] = value


def put_q(outs, k, value):
    outs[0][0, :, k * WQ : k * WQ + WQ] = value


def error_squares(place, total, far, targets, low, high, out_shape, out_spec, put):
    width = high - low
    return pl.pallas_call(
        lambda *refs: square_kernel(low, high, put, *refs),
        grid_spec=pltpu.PrefetchScalarGridSpec(
            num_scalar_prefetch=1,
            grid=(2,),
            in_specs=[
                pl.BlockSpec((64, 4 * width), lambda j, s: (0, j)),
                pl.BlockSpec((64, 4 * width), lambda j, s: (0, j)),
                pl.BlockSpec((64, 4 * WIDE), lambda j, s: (s[3] * 4 + s[2], j)),
            ],
            out_specs=out_spec,
        ),
        out_shape=out_shape,
        compiler_params=pltpu.CompilerParams(vmem_limit_bytes=VMEM),
        cost_estimate=SMALL,
    )(place, total, far, targets)


def place_tokens(parts, scratch):
    for c, part in enumerate(parts):
        for place in range(4):
            row = c * 256 + place * 64
            for k in range(scratch.shape[0]):
                scratch[k, row : row + 64, :] = part[place, k]


def sums(units, weights, squares, number):
    numerator = denominator = None
    for k in range(number):
        fisher = jnp.dot(units[k], squares(k), preferred_element_type=F32) * (1.0 / TOK)
        weighted = (fisher * weights(k).astype(F32)).astype(BF).astype(F32)
        term = fisher.astype(BF).astype(F32)
        numerator = weighted if numerator is None else numerator + weighted
        denominator = term if denominator is None else denominator + term
    return numerator, denominator


def set_p_kernel(counts, place_ref, own_units, own, *refs):
    refs = list(refs)
    groups = []
    for count in counts:
        groups.append(jnp.concatenate([ref[...] for ref in refs[:count]], axis=1))
        del refs[:count]
    parts, (out_ref, scratch) = refs[:2], refs[2:]

    @pl.when(pl.program_id(0) == 0)
    def _():
        place_tokens(parts, scratch)

    units, weights = [own_units[...]] + groups[:3], [own[:, :WP]] + groups[3:]
    numerator, denominator = sums(units, lambda k: weights[k], lambda k: scratch[k], 4)
    out_ref[0] = numerator.astype(out_ref.dtype)
    out_ref[1] = denominator.astype(out_ref.dtype)


def set_p(place, squares, projection, moved, parts, dy, dtype, first=0, count=4):
    tall = 224
    pieces = [piece for group in moved for piece in group]
    return pl.pallas_call(
        lambda *refs: set_p_kernel([len(group) for group in moved], *refs),
        grid_spec=pltpu.PrefetchScalarGridSpec(
            num_scalar_prefetch=1,
            grid=(count,),
            in_specs=[
                pl.BlockSpec((tall, TOK), lambda u, s: (u + first, 0)),
                pl.BlockSpec((tall, WIDE), lambda u, s: (u + first, lax.rem(s[0] + dy, 2) * 4 + s[1])),
            ]
            + [pl.BlockSpec((tall, width), lambda u, s, i=i: (u + first, i)) for _, width, i in pieces]
            + [pl.BlockSpec((4, 4, 64, WP), lambda u, s: (0, 0, 0, dy))] * 2,
            out_specs=pl.BlockSpec((2, tall, WP), lambda u, s: (0, u, 0)),
            scratch_shapes=[pltpu.VMEM((4, TOK, WP), BF)],
        ),
        out_shape=shape(2, count * tall, WP, dtype=dtype),
        compiler_params=pltpu.CompilerParams(vmem_limit_bytes=VMEM),
        cost_estimate=SMALL,
    )(place, squares, projection, *[array for array, _, _ in pieces], *parts)


def set_q_kernel(place_ref, own_units, far_units, own_0, own_1, own_2, own_3, far_weights, *refs):
    own_weights = (own_0, own_1, own_2, own_3)
    parts, outs, scratch = refs[:2], refs[2:6], refs[6]

    @pl.when(pl.program_id(0) == 0)
    def _():
        place_tokens(parts, scratch)

    for dz in (1, 2, 3, 0):
        columns = slice(dz * WQ, dz * WQ + WQ)
        weights = (own_weights[dz][...], far_weights[:, columns])
        numerator, denominator = sums(
            [own_units[...], far_units[...]], lambda k: weights[k], lambda k: scratch[k, :, columns], 2
        )
        outs[dz][0] = numerator.astype(outs[dz].dtype)
        outs[dz][1] = denominator.astype(outs[dz].dtype)


def set_q(place, units, far_units, projection, far, parts):
    tall = 224

    def own(dz):
        return pl.BlockSpec((tall, WQ), lambda u, s: (u, (s[0] * 4 + lax.rem(s[1] + dz, 4)) * (WIDE // WQ) + WP // WQ))

    return pl.pallas_call(
        set_q_kernel,
        grid_spec=pltpu.PrefetchScalarGridSpec(
            num_scalar_prefetch=1,
            grid=(UNITS // tall,),
            in_specs=[
                pl.BlockSpec((tall, TOK), lambda u, s: (u, 0)),
                pl.BlockSpec((tall, TOK), lambda u, s: (u, 0)),
            ]
            + [own(dz) for dz in range(4)]
            + [pl.BlockSpec((tall, 4 * WQ), lambda u, s: (u, 0))]
            + [pl.BlockSpec((4, 2, 64, 4 * WQ), lambda u, s: (0, 0, 0, 0))] * 2,
            out_specs=[pl.BlockSpec((2, tall, WQ), lambda u, s: (0, u, 0))] * 4,
            scratch_shapes=[pltpu.VMEM((2, TOK, 4 * WQ), BF)],
        ),
        out_shape=[shape(2, UNITS, WQ)] * 4,
        compiler_params=pltpu.CompilerParams(vmem_limit_bytes=VMEM),
        cost_estimate=SMALL,
    )(place, units, far_units, projection, projection, projection, projection, far, *parts)


def quotient_kernel(n_given, *refs):
    out_ref = refs[-1]

    def total(i):
        value = refs[0][i].astype(F32)
        for ref in refs[1 : -1 - n_given]:
            value = value + ref[i].astype(F32)
        return value

    out_ref[...] = total(0) / (total(1) + 1e-06)


def quotient(columns, terms, before=None, first=0, count=4):
    tall = 224
    width = columns.stop - columns.start
    place = columns.start // width
    given = [] if before is None else [before]
    return pl.pallas_call(
        lambda *refs: quotient_kernel(len(given), *refs),
        grid=(count,),
        in_specs=[
            pl.BlockSpec((2, tall, width), lambda u, start=first * (term.shape[1] == UNITS): (0, u + start, 0))
            for term in terms
        ]
        + [pl.BlockSpec(memory_space=pl.ANY)] * len(given),
        out_specs=pl.BlockSpec((tall, width), lambda u: (u + first, place)),
        out_shape=shape(UNITS, WIDE, dtype=F32),
        input_output_aliases={len(terms): 0} if given else {},
        compiler_params=pltpu.CompilerParams(vmem_limit_bytes=VMEM),
        cost_estimate=SMALL,
    )(*terms, *given)


def body(token_rows, gate_cache, up_cache, down_weight, targets):
    y, z, x, core = (lax.axis_index(name) for name in ("y_lo", "z", "x", "core"))
    place = jnp.stack([y, z, x, core]).astype(jnp.int32)
    projection = down_weight[0]

    def send(value, axis, k=1):
        return lax.ppermute(value, axis, shift(k) if axis in ("z", "x") else SWAP)

    together = lax.optimization_barrier

    hidden, squares = make_hidden(place, token_rows, gate_cache[0], up_cache[0])

    own_p, other_p = partial_outputs(hidden, projection, 0, WP)
    other_p, squares = together((other_p, squares))
    side, one, three = cut(
        cut_first_kernel, place, [squares], projection,
        [(0, 1), (0, 3), (1, 0), (1, 1), (1, 2), (1, 3)], [4 * WQ, WP + WN + TOK, WP + WN + TOK],
    )
    one, three, side = send(one, "z", 1), send(three, "z", 3), send(side, "y_lo")

    def pair(own, other):
        both = (own.astype(F32) + send(other, "core").astype(F32)).astype(BF)
        return both.reshape(4, 64, -1)

    def over_x(blocks):
        return lax.all_to_all(blocks, "x", 0, 0, tiled=True)

    def total(blocks):
        return jnp.sum(blocks.astype(F32), axis=0).astype(BF)

    def gathered(part):
        return over_x(jnp.broadcast_to(part[None], (4,) + part.shape))

    pair_p, hidden = together((pair(own_p, other_p), hidden))
    blocks_p = over_x(pair_p)
    pair_q = pair(*partial_outputs(hidden, projection, WP, WIDE))
    blocks_p, pair_q = together((blocks_p, pair_q))
    total_p = total(blocks_p)
    total_p, side = together((total_p, side))
    far_p = send(total_p, "y_hi")
    blocks_q = over_x(pair_q)
    squares_p = error_squares(
        place, total_p, far_p, targets[0], 0, WP, [shape(64, 2 * WP)] * 4,
        [pl.BlockSpec((64, WP), lambda j, s: (0, lax.rem(j + s[0], 2)))] * 4, put_p,
    )
    late_1, early_2, late_2, late_3, far_2 = cut(
        cut_second_kernel, place, [], projection,
        [(0, 1), (0, 2), (0, 3), (1, 2)], [WP - WN, WN2, WP - WN2, WP - WN, WP],
    )
    squares_p, one, three, blocks_q, far_2, early_2, late = together(
        (squares_p, one, three, blocks_q, far_2, early_2, (late_1, late_2, late_3))
    )
    total_q = total(blocks_q)
    far_q = send(total_q, "y_hi")
    mine_p = jnp.stack([squares_p[0]] + [send(squares_p[k], "z", k) for k in (1, 2, 3)])
    middle = WP + TOK // 2
    u_2 = (one[:, WP:middle], three[:, middle : WP + TOK])
    mine_p, far_2, u_2, squares_late = together((mine_p, far_2, u_2, squares))

    u_2 = (send(u_2[0], "z", 1), send(u_2[1], "z", 3))
    far_2, u_side = send(far_2, "z", 2), send(squares_late, "y_lo")
    row_p = gathered(mine_p)
    squares_q = error_squares(
        place, total_q, far_q, targets[0], WP, WIDE, shape(2, 64, 4 * WQ),
        pl.BlockSpec((1, 64, 4 * WQ), lambda j, s: (lax.rem(j + s[0], 2), 0, 0)), put_q,
    )
    mine_q = jnp.stack([squares_q[0], send(squares_q[1], "y_lo")])
    row_p, far_2, u_2, u_side, mine_q, early_2, late = together(
        (row_p, far_2, u_2, u_side, mine_q, early_2, late)
    )

    half = TOK // 2

    def units_in(array):
        return [(array, half, WP // half), (array, half, WP // half + 1)]

    def near_in(array, late):
        return [(array, WN, (WP + TOK) // WN), (late, WP - WN, 0)]

    units = [units_in(one), [(u, half, 0) for u in u_2], units_in(three)]
    fars = [[(array, WP, 0)] for array in (one, far_2, three)]
    early_2 = send(early_2, "z", 2)
    parts_p = [row_p, send(row_p, "core")]
    p_far = send(set_p(place, squares, projection, units + fars, parts_p, 1, BF), "y_lo")
    row_q, early_2, late = together((gathered(mine_q), early_2, late))
    late = [send(piece, "z", k + 1) for k, piece in enumerate(late)]
    parts_q = [row_q, send(row_q, "core")]
    q_sums = set_q(place, squares, u_side, projection, side, parts_q)
    q_own, *q_send = q_sums
    q_send[1], late = together((q_send[1], late))
    q_far = [send(q, "z", k + 1) for k, q in enumerate(q_send)]
    nears = [
        near_in(one, late[0]),
        [(early_2, WN2, 0), (late[1], WP - WN2, 0)],
        near_in(three, late[2]),
    ]
    p_own = set_p(place, squares, projection, units + nears, parts_p, 0, BF)
    merged = quotient(slice(0, WP), [p_own, p_far])
    return quotient(slice(WP, WIDE), [q_own, *q_far], merged)


def solution(mesh):
    cut = Mesh(mesh.devices.reshape(2, 4, 2, 4, 2), ("y_lo", "z", "y_hi", "x", "core"))
    ft, tp = ("y_lo", "z"), ("y_hi", "x", "core")
    placed = (P(ft, None), P(ft, None, tp), P(ft, None, tp), P(ft, tp, None), P(ft, None, None))
    return jax.shard_map(body, mesh=cut, in_specs=placed, out_specs=P(tp, ft), check_vma=False)
```

```python
import math

import jax
import jax.numpy as jnp
from jax import lax
from jax.experimental import pallas as pl
from jax.experimental.pallas import tpu as pltpu
from jax.sharding import Mesh
from jax.sharding import PartitionSpec as P

FF = 14336
TOK = 512
POOL = 1024
UNITS = 896
D = 8192
WIDE = 1024
WP = 768
WQ = WIDE - WP
WN = 640
WN2 = 640
VMEM = 56 * 2**20
SHRINK = 1.0 / math.sqrt(FF)
SWAP = [(0, 1), (1, 0)]
BF = jnp.bfloat16
F32 = jnp.float32
SMALL = pl.CostEstimate(flops=1, bytes_accessed=1, transcendentals=0)


def shift(k):
    return [(i, (i + k) % 4) for i in range(4)]


def shape(*dims, dtype=BF):
    return jax.ShapeDtypeStruct(dims, dtype)


def hidden_kernel(place_ref, rows_ref, gate_ref, up_ref, hidden_ref, squares_ref):
    rows = rows_ref[...]
    other = jnp.concatenate([rows[:, TOK // 2 :], rows[:, : TOK // 2]], axis=1)
    rows = jnp.where(place_ref[3] == 1, other, rows)
    pool = lax.broadcasted_iota(jnp.int32, (POOL, TOK), 0)
    pick = jnp.where(rows == pool, 1.0, 0.0).T.astype(BF)
    gate = jnp.dot(pick, gate_ref[...], preferred_element_type=F32)
    up = jnp.dot(pick, up_ref[...], preferred_element_type=F32)
    hidden = (gate / (1.0 + jnp.exp(-gate)) * up).astype(BF)
    hidden_ref[...] = hidden
    wide = hidden.astype(F32)
    squares_ref[...] = (wide * wide).T.astype(BF)


def make_hidden(place, rows, gate, up):
    return pl.pallas_call(
        hidden_kernel,
        grid_spec=pltpu.PrefetchScalarGridSpec(
            num_scalar_prefetch=1,
            grid=(1,),
            in_specs=[
                pl.BlockSpec((1, TOK), lambda i, s: (0, 0)),
                pl.BlockSpec((POOL, UNITS), lambda i, s: (0, 0)),
                pl.BlockSpec((POOL, UNITS), lambda i, s: (0, 0)),
            ],
            out_specs=[
                pl.BlockSpec((TOK, UNITS), lambda i, s: (0, 0)),
                pl.BlockSpec((UNITS, TOK), lambda i, s: (0, 0)),
            ],
        ),
        out_shape=[shape(TOK, UNITS), shape(UNITS, TOK)],
        compiler_params=pltpu.CompilerParams(vmem_limit_bytes=VMEM),
        cost_estimate=SMALL,
    )(place, rows, gate, up)


def cut_first_kernel(place_ref, squares_ref, near_1, near_3, far_0, far_1, far_2, far_3, side, one, three):
    squares = squares_ref[...]
    for out, far, near in ((one, far_1, near_1), (three, far_3, near_3)):
        out[:, :WP] = far[:, :WP]
        out[:, WP : WP + TOK] = squares
        out[:, WP + TOK :] = near[:, :WN]
    for dz, far in enumerate((far_0, far_1, far_2, far_3)):
        side[:, dz * WQ : dz * WQ + WQ] = far[:, WP:]


def cut_second_kernel(place_ref, near_1, near_2, near_3, far_2, late_1, early_2, late_2, late_3, far_two):
    late_1[...] = near_1[:, WN:WP]
    late_3[...] = near_3[:, WN:WP]
    early_2[...] = near_2[:, :WN2]
    late_2[...] = near_2[:, WN2:WP]
    far_two[...] = far_2[:, :WP]


def cut(kernel, place, extra, projection, places, widths):
    step = 224

    def columns(dy, dz):
        return pl.BlockSpec((step, WIDE), lambda i, s: (i, lax.rem(s[0] + dy, 2) * 4 + lax.rem(s[1] + dz, 4)))

    def rows_of(width):
        return pl.BlockSpec((step, width), lambda i, s: (i, 0))

    return pl.pallas_call(
        kernel,
        grid_spec=pltpu.PrefetchScalarGridSpec(
            num_scalar_prefetch=1,
            grid=(UNITS // step,),
            in_specs=[rows_of(TOK)] * len(extra) + [columns(dy, dz) for dy, dz in places],
            out_specs=[rows_of(width) for width in widths],
        ),
        out_shape=[shape(UNITS, width) for width in widths],
        compiler_params=pltpu.CompilerParams(vmem_limit_bytes=50 * 2**20),
        cost_estimate=SMALL,
    )(place, *extra, *[projection] * len(places))


def partial_kernel(hidden_ref, *refs):
    hidden = hidden_ref[...]
    *streams, own, other = refs
    for i, stream in enumerate(streams):
        columns = slice(i * WQ, i * WQ + WQ)
        product = (jnp.dot(hidden, stream[...], preferred_element_type=F32) * SHRINK).astype(BF)
        own[:, columns] = product[:256]
        other[:, columns] = product[256:]


def partial_outputs(hidden, projection, low, high):
    width = high - low
    streams = [
        pl.BlockSpec((UNITS, WQ), lambda j, i=i: (0, j * (WIDE // WQ) + i)) for i in range(low // WQ, high // WQ)
    ]
    return pl.pallas_call(
        partial_kernel,
        grid=(8,),
        in_specs=[pl.BlockSpec((TOK, UNITS), lambda j: (0, 0)), *streams],
        out_specs=[pl.BlockSpec((256, width), lambda j: (0, j))] * 2,
        out_shape=[shape(256, 8 * width)] * 2,
        compiler_params=pltpu.CompilerParams(vmem_limit_bytes=50 * 2**20),
        cost_estimate=SMALL,
    )(hidden, *[projection] * len(streams))


def square_kernel(low, high, put, place_ref, total_ref, far_ref, targets_ref, *outs):
    width = high - low
    for k in range(4):
        place = lax.rem(place_ref[1] + k, 4)
        columns = pl.ds(pl.multiple_of(place * width, 128), width)
        outputs = total_ref[:, columns].astype(F32) + far_ref[:, columns].astype(F32)
        wanted = targets_ref[:, pl.ds(pl.multiple_of(place * WIDE + low, 128), width)].astype(F32)
        errors = (outputs - wanted).astype(BF).astype(F32)
        put(outs, k, (errors * errors).astype(BF))


def put_p(outs, k, value):
    outs[k][...] = value


def put_q(outs, k, value):
    outs[0][0, :, k * WQ : k * WQ + WQ] = value


def error_squares(place, total, far, targets, low, high, out_shape, out_spec, put):
    width = high - low
    return pl.pallas_call(
        lambda *refs: square_kernel(low, high, put, *refs),
        grid_spec=pltpu.PrefetchScalarGridSpec(
            num_scalar_prefetch=1,
            grid=(2,),
            in_specs=[
                pl.BlockSpec((64, 4 * width), lambda j, s: (0, j)),
                pl.BlockSpec((64, 4 * width), lambda j, s: (0, j)),
                pl.BlockSpec((64, 4 * WIDE), lambda j, s: (s[3] * 4 + s[2], j)),
            ],
            out_specs=out_spec,
        ),
        out_shape=out_shape,
        compiler_params=pltpu.CompilerParams(vmem_limit_bytes=VMEM),
        cost_estimate=SMALL,
    )(place, total, far, targets)


def place_tokens(parts, scratch):
    for c, part in enumerate(parts):
        for place in range(4):
            row = c * 256 + place * 64
            for k in range(scratch.shape[0]):
                scratch[k, row : row + 64, :] = part[place, k]


def sums(units, weights, squares, number):
    numerator = denominator = None
    for k in range(number):
        fisher = jnp.dot(units[k], squares(k), preferred_element_type=F32)
        weighted = fisher * weights(k).astype(F32)
        numerator = weighted if numerator is None else numerator + weighted
        denominator = fisher if denominator is None else denominator + fisher
    return numerator, denominator


def set_p_kernel(counts, place_ref, own_units, own, *refs):
    refs = list(refs)
    groups = []
    for count in counts:
        groups.append(jnp.concatenate([ref[...] for ref in refs[:count]], axis=1))
        del refs[:count]
    parts, (out_ref, scratch) = refs[:2], refs[2:]

    @pl.when(pl.program_id(0) == 0)
    def _():
        place_tokens(parts, scratch)

    units, weights = [own_units[...]] + groups[:3], [own[:, :WP]] + groups[3:]
    numerator, denominator = sums(units, lambda k: weights[k], lambda k: scratch[k], 4)
    out_ref[0] = numerator.astype(out_ref.dtype)
    out_ref[1] = denominator.astype(out_ref.dtype)


def set_p(place, squares, projection, moved, parts, dy, dtype):
    tall = 224
    pieces = [piece for group in moved for piece in group]
    return pl.pallas_call(
        lambda *refs: set_p_kernel([len(group) for group in moved], *refs),
        grid_spec=pltpu.PrefetchScalarGridSpec(
            num_scalar_prefetch=1,
            grid=(UNITS // tall,),
            in_specs=[
                pl.BlockSpec((tall, TOK), lambda u, s: (u, 0)),
                pl.BlockSpec((tall, WIDE), lambda u, s: (u, lax.rem(s[0] + dy, 2) * 4 + s[1])),
            ]
            + [pl.BlockSpec((tall, width), lambda u, s, i=i: (u, i)) for _, width, i in pieces]
            + [pl.BlockSpec((4, 4, 64, WP), lambda u, s: (0, 0, 0, dy))] * 2,
            out_specs=pl.BlockSpec((2, tall, WP), lambda u, s: (0, u, 0)),
            scratch_shapes=[pltpu.VMEM((4, TOK, WP), BF)],
        ),
        out_shape=shape(2, UNITS, WP, dtype=dtype),
        compiler_params=pltpu.CompilerParams(vmem_limit_bytes=VMEM),
        cost_estimate=SMALL,
    )(place, squares, projection, *[array for array, _, _ in pieces], *parts)


def set_q_kernel(place_ref, own_units, far_units, own_0, own_1, own_2, own_3, far_weights, *refs):
    own_weights = (own_0, own_1, own_2, own_3)
    parts, outs, scratch = refs[:2], refs[2:6], refs[6]

    @pl.when(pl.program_id(0) == 0)
    def _():
        place_tokens(parts, scratch)

    for dz in (1, 2, 3, 0):
        columns = slice(dz * WQ, dz * WQ + WQ)
        weights = (own_weights[dz][...], far_weights[:, columns])
        numerator, denominator = sums(
            [own_units[...], far_units[...]], lambda k: weights[k], lambda k: scratch[k, :, columns], 2
        )
        outs[dz][0] = numerator.astype(outs[dz].dtype)
        outs[dz][1] = denominator.astype(outs[dz].dtype)


def set_q(place, units, far_units, projection, far, parts):
    tall = 224

    def own(dz):
        return pl.BlockSpec((tall, WQ), lambda u, s: (u, (s[0] * 4 + lax.rem(s[1] + dz, 4)) * (WIDE // WQ) + WP // WQ))

    return pl.pallas_call(
        set_q_kernel,
        grid_spec=pltpu.PrefetchScalarGridSpec(
            num_scalar_prefetch=1,
            grid=(UNITS // tall,),
            in_specs=[
                pl.BlockSpec((tall, TOK), lambda u, s: (u, 0)),
                pl.BlockSpec((tall, TOK), lambda u, s: (u, 0)),
            ]
            + [own(dz) for dz in range(4)]
            + [pl.BlockSpec((tall, 4 * WQ), lambda u, s: (u, 0))]
            + [pl.BlockSpec((4, 2, 64, 4 * WQ), lambda u, s: (0, 0, 0, 0))] * 2,
            out_specs=[pl.BlockSpec((2, tall, WQ), lambda u, s: (0, u, 0))] * 4,
            scratch_shapes=[pltpu.VMEM((2, TOK, 4 * WQ), BF)],
        ),
        out_shape=[shape(2, UNITS, WQ)] * 4,
        compiler_params=pltpu.CompilerParams(vmem_limit_bytes=VMEM),
        cost_estimate=SMALL,
    )(place, units, far_units, projection, projection, projection, projection, far, *parts)


def quotient_kernel(n_given, *refs):
    out_ref = refs[-1]

    def total(i):
        value = refs[0][i].astype(F32)
        for ref in refs[1 : -1 - n_given]:
            value = value + ref[i].astype(F32)
        return value

    out_ref[...] = total(0) / (total(1) + TOK * 1e-06)


def quotient(columns, terms, before=None, tall=224):
    width = columns.stop - columns.start
    place = columns.start // width
    given = [] if before is None else [before]
    return pl.pallas_call(
        lambda *refs: quotient_kernel(len(given), *refs),
        grid=(UNITS // tall,),
        in_specs=[pl.BlockSpec((2, tall, width), lambda u: (0, u, 0))] * len(terms)
        + [pl.BlockSpec(memory_space=pl.ANY)] * len(given),
        out_specs=pl.BlockSpec((tall, width), lambda u: (u, place)),
        out_shape=shape(UNITS, WIDE, dtype=F32),
        input_output_aliases={len(terms): 0} if given else {},
        compiler_params=pltpu.CompilerParams(vmem_limit_bytes=VMEM),
        cost_estimate=SMALL,
    )(*terms, *given)


def body(token_rows, gate_cache, up_cache, down_weight, targets):
    y, z, x, core = (lax.axis_index(name) for name in ("y_lo", "z", "x", "core"))
    place = jnp.stack([y, z, x, core]).astype(jnp.int32)
    projection = down_weight[0]

    def send(value, axis, k=1):
        return lax.ppermute(value, axis, shift(k) if axis in ("z", "x") else SWAP)

    together = lax.optimization_barrier

    hidden, squares = make_hidden(place, token_rows, gate_cache[0], up_cache[0])

    own_p, other_p = partial_outputs(hidden, projection, 0, WP)
    other_p, squares = together((other_p, squares))
    side, one, three = cut(
        cut_first_kernel, place, [squares], projection,
        [(0, 1), (0, 3), (1, 0), (1, 1), (1, 2), (1, 3)], [4 * WQ, WP + WN + TOK, WP + WN + TOK],
    )
    one, three, side = send(one, "z", 1), send(three, "z", 3), send(side, "y_lo")

    def pair(own, other):
        both = (own.astype(F32) + send(other, "core").astype(F32)).astype(BF)
        return both.reshape(4, 64, -1)

    def over_x(blocks):
        return lax.all_to_all(blocks, "x", 0, 0, tiled=True)

    def total(blocks):
        return jnp.sum(blocks.astype(F32), axis=0).astype(BF)

    def four(part):
        return jnp.broadcast_to(part[None], (4,) + part.shape)

    pair_p, hidden = together((pair(own_p, other_p), hidden))
    blocks_p = over_x(pair_p)
    pair_q = pair(*partial_outputs(hidden, projection, WP, WIDE))
    blocks_p, pair_q = together((blocks_p, pair_q))
    total_p = total(blocks_p)
    total_p, side = together((total_p, side))
    far_p = send(total_p, "y_hi")
    blocks_q = over_x(pair_q)
    squares_p = error_squares(
        place, total_p, far_p, targets[0], 0, WP, [shape(64, 2 * WP)] * 4,
        [pl.BlockSpec((64, WP), lambda j, s: (0, lax.rem(j + s[0], 2)))] * 4, put_p,
    )
    late_1, early_2, late_2, late_3, far_2 = cut(
        cut_second_kernel, place, [], projection,
        [(0, 1), (0, 2), (0, 3), (1, 2)], [WP - WN, WN2, WP - WN2, WP - WN, WP],
    )
    squares_p, one, three, blocks_q, far_2, early_2, late = together(
        (squares_p, one, three, blocks_q, far_2, early_2, (late_1, late_2, late_3))
    )
    total_q = total(blocks_q)
    far_q = send(total_q, "y_hi")
    mine_p = jnp.stack([squares_p[0]] + [send(squares_p[k], "z", k) for k in (1, 2, 3)])
    middle = WP + TOK // 2
    u_2 = (one[:, WP:middle], three[:, middle : WP + TOK])
    mine_p, far_2, u_2, squares_late = together((mine_p, far_2, u_2, squares))

    u_2 = (send(u_2[0], "z", 1), send(u_2[1], "z", 3))
    far_2, u_side = send(far_2, "z", 2), send(squares_late, "y_lo")
    row_p = over_x(four(mine_p))
    squares_q = error_squares(
        place, total_q, far_q, targets[0], WP, WIDE, shape(2, 64, 4 * WQ),
        pl.BlockSpec((1, 64, 4 * WQ), lambda j, s: (lax.rem(j + s[0], 2), 0, 0)), put_q,
    )
    mine_q = jnp.stack([squares_q[0], send(squares_q[1], "y_lo")])
    row_p, far_2, u_2, u_side, mine_q, early_2, late = together(
        (row_p, far_2, u_2, u_side, mine_q, early_2, late)
    )

    half = TOK // 2

    def units_in(array):
        return [(array, half, WP // half), (array, half, WP // half + 1)]

    def near_in(array, late):
        return [(array, WN, (WP + TOK) // WN), (late, WP - WN, 0)]

    units = [units_in(one), [(u, half, 0) for u in u_2], units_in(three)]
    fars = [[(array, WP, 0)] for array in (one, far_2, three)]
    early_2 = send(early_2, "z", 2)
    parts_p = [row_p, send(row_p, "core")]
    p_far = send(set_p(place, squares, projection, units + fars, parts_p, 1, BF), "y_lo")
    row_q, early_2, late = together((over_x(four(mine_q)), early_2, late))
    late = [send(piece, "z", k + 1) for k, piece in enumerate(late)]
    parts_q = [row_q, send(row_q, "core")]
    q_sums = set_q(place, squares, u_side, projection, side, parts_q)
    q_own, *q_send = q_sums
    q_send[1], late = together((q_send[1], late))
    q_far = [send(q, "z", k + 1) for k, q in enumerate(q_send)]
    nears = [
        near_in(one, late[0]),
        [(early_2, WN2, 0), (late[1], WP - WN2, 0)],
        near_in(three, late[2]),
    ]
    p_own = set_p(place, squares, projection, units + nears, parts_p, 0, BF)
    merged = quotient(slice(0, WP), [p_own, p_far])
    return quotient(slice(WP, WIDE), [q_own, *q_far], merged, 448)


def solution(mesh):
    cut = Mesh(mesh.devices.reshape(2, 4, 2, 4, 2), ("y_lo", "z", "y_hi", "x", "core"))
    ft, tp = ("y_lo", "z"), ("y_hi", "x", "core")
    placed = (P(ft, None), P(ft, None, tp), P(ft, None, tp), P(ft, tp, None), P(ft, None, None))
    return jax.shard_map(body, mesh=cut, in_specs=placed, out_specs=P(tp, ft), check_vma=False)
```

```python
import math

import jax
import jax.numpy as jnp
from jax import lax
from jax.experimental import pallas as pl
from jax.experimental.pallas import tpu as pltpu
from jax.sharding import Mesh
from jax.sharding import PartitionSpec as P

FF = 14336
TOK = 512
POOL = 1024
UNITS = 896
D = 8192
WIDE = 1024
WP = 768
WQ = WIDE - WP
WN = 640
WN2 = 640
VMEM = 56 * 2**20
SHRINK = 1.0 / math.sqrt(FF)
SWAP = [(0, 1), (1, 0)]
BF = jnp.bfloat16
F32 = jnp.float32
SMALL = pl.CostEstimate(flops=1, bytes_accessed=1, transcendentals=0)


def shift(k):
    return [(i, (i + k) % 4) for i in range(4)]


def shape(*dims, dtype=BF):
    return jax.ShapeDtypeStruct(dims, dtype)


def hidden_kernel(place_ref, rows_ref, gate_ref, up_ref, hidden_ref, squares_ref):
    rows = rows_ref[...]
    other = jnp.concatenate([rows[:, TOK // 2 :], rows[:, : TOK // 2]], axis=1)
    rows = jnp.where(place_ref[3] == 1, other, rows)
    pool = lax.broadcasted_iota(jnp.int32, (POOL, TOK), 0)
    pick = jnp.where(rows == pool, 1.0, 0.0).T.astype(BF)
    gate = jnp.dot(pick, gate_ref[...], preferred_element_type=F32)
    up = jnp.dot(pick, up_ref[...], preferred_element_type=F32)
    hidden = (gate / (1.0 + jnp.exp(-gate)) * up).astype(BF)
    hidden_ref[...] = hidden
    wide = hidden.astype(F32)
    squares_ref[...] = (wide * wide).T.astype(BF)


def make_hidden(place, rows, gate, up):
    return pl.pallas_call(
        hidden_kernel,
        grid_spec=pltpu.PrefetchScalarGridSpec(
            num_scalar_prefetch=1,
            grid=(1,),
            in_specs=[
                pl.BlockSpec((1, TOK), lambda i, s: (0, 0)),
                pl.BlockSpec((POOL, UNITS), lambda i, s: (0, 0)),
                pl.BlockSpec((POOL, UNITS), lambda i, s: (0, 0)),
            ],
            out_specs=[
                pl.BlockSpec((TOK, UNITS), lambda i, s: (0, 0)),
                pl.BlockSpec((UNITS, TOK), lambda i, s: (0, 0)),
            ],
        ),
        out_shape=[shape(TOK, UNITS), shape(UNITS, TOK)],
        compiler_params=pltpu.CompilerParams(vmem_limit_bytes=VMEM),
        cost_estimate=SMALL,
    )(place, rows, gate, up)


def cut_first_kernel(place_ref, squares_ref, near_1, near_3, far_0, far_1, far_2, far_3, side, one, three):
    squares = squares_ref[...]
    for out, far, near in ((one, far_1, near_1), (three, far_3, near_3)):
        out[:, :WP] = far[:, :WP]
        out[:, WP : WP + TOK] = squares
        out[:, WP + TOK :] = near[:, :WN]
    for dz, far in enumerate((far_0, far_1, far_2, far_3)):
        side[:, dz * WQ : dz * WQ + WQ] = far[:, WP:]


def cut_second_kernel(place_ref, near_1, near_2, near_3, far_2, late_1, early_2, late_2, late_3, far_two):
    late_1[...] = near_1[:, WN:WP]
    late_3[...] = near_3[:, WN:WP]
    early_2[...] = near_2[:, :WN2]
    late_2[...] = near_2[:, WN2:WP]
    far_two[...] = far_2[:, :WP]


def cut(kernel, place, extra, projection, places, widths):
    step = 224

    def columns(dy, dz):
        return pl.BlockSpec((step, WIDE), lambda i, s: (i, lax.rem(s[0] + dy, 2) * 4 + lax.rem(s[1] + dz, 4)))

    def rows_of(width):
        return pl.BlockSpec((step, width), lambda i, s: (i, 0))

    return pl.pallas_call(
        kernel,
        grid_spec=pltpu.PrefetchScalarGridSpec(
            num_scalar_prefetch=1,
            grid=(UNITS // step,),
            in_specs=[rows_of(TOK)] * len(extra) + [columns(dy, dz) for dy, dz in places],
            out_specs=[rows_of(width) for width in widths],
        ),
        out_shape=[shape(UNITS, width) for width in widths],
        compiler_params=pltpu.CompilerParams(vmem_limit_bytes=50 * 2**20),
        cost_estimate=SMALL,
    )(place, *extra, *[projection] * len(places))


def partial_kernel(hidden_ref, *refs):
    hidden = hidden_ref[...]
    *streams, own, other = refs
    for i, stream in enumerate(streams):
        columns = slice(i * WQ, i * WQ + WQ)
        product = (jnp.dot(hidden, stream[...], preferred_element_type=F32) * SHRINK).astype(BF)
        own[:, columns] = product[:256]
        other[:, columns] = product[256:]


def partial_outputs(hidden, projection, low, high):
    width = high - low
    streams = [
        pl.BlockSpec((UNITS, WQ), lambda j, i=i: (0, j * (WIDE // WQ) + i)) for i in range(low // WQ, high // WQ)
    ]
    return pl.pallas_call(
        partial_kernel,
        grid=(8,),
        in_specs=[pl.BlockSpec((TOK, UNITS), lambda j: (0, 0)), *streams],
        out_specs=[pl.BlockSpec((256, width), lambda j: (0, j))] * 2,
        out_shape=[shape(256, 8 * width)] * 2,
        compiler_params=pltpu.CompilerParams(vmem_limit_bytes=50 * 2**20),
        cost_estimate=SMALL,
    )(hidden, *[projection] * len(streams))


def square_kernel(low, high, put, place_ref, total_ref, far_ref, targets_ref, *outs):
    width = high - low
    for k in range(4):
        place = lax.rem(place_ref[1] + k, 4)
        columns = pl.ds(pl.multiple_of(place * width, 128), width)
        outputs = total_ref[:, columns].astype(F32) + far_ref[:, columns].astype(F32)
        wanted = targets_ref[:, pl.ds(pl.multiple_of(place * WIDE + low, 128), width)].astype(F32)
        errors = (outputs - wanted).astype(BF).astype(F32)
        put(outs, k, (errors * errors).astype(BF))


def put_p(outs, k, value):
    outs[k][...] = value


def put_q(outs, k, value):
    outs[0][0, :, k * WQ : k * WQ + WQ] = value


def error_squares(place, total, far, targets, low, high, out_shape, out_spec, put):
    width = high - low
    return pl.pallas_call(
        lambda *refs: square_kernel(low, high, put, *refs),
        grid_spec=pltpu.PrefetchScalarGridSpec(
            num_scalar_prefetch=1,
            grid=(2,),
            in_specs=[
                pl.BlockSpec((64, 4 * width), lambda j, s: (0, j)),
                pl.BlockSpec((64, 4 * width), lambda j, s: (0, j)),
                pl.BlockSpec((64, 4 * WIDE), lambda j, s: (s[3] * 4 + s[2], j)),
            ],
            out_specs=out_spec,
        ),
        out_shape=out_shape,
        compiler_params=pltpu.CompilerParams(vmem_limit_bytes=VMEM),
        cost_estimate=SMALL,
    )(place, total, far, targets)


def place_tokens(parts, scratch):
    for c, part in enumerate(parts):
        for place in range(4):
            row = c * 256 + place * 64
            for k in range(scratch.shape[0]):
                scratch[k, row : row + 64, :] = part[place, k]


def sums(units, weights, squares, number):
    numerator = denominator = None
    for k in range(number):
        fisher = jnp.dot(units[k], squares(k), preferred_element_type=F32)
        weighted = fisher * weights(k).astype(F32)
        numerator = weighted if numerator is None else numerator + weighted
        denominator = fisher if denominator is None else denominator + fisher
    return numerator, denominator


def set_p_kernel(counts, place_ref, own_units, own, *refs):
    refs = list(refs)
    groups = []
    for count in counts:
        groups.append(jnp.concatenate([ref[...] for ref in refs[:count]], axis=1))
        del refs[:count]
    parts, (out_ref, scratch) = refs[:2], refs[2:]

    @pl.when(pl.program_id(0) == 0)
    def _():
        place_tokens(parts, scratch)

    units, weights = [own_units[...]] + groups[:3], [own[:, :WP]] + groups[3:]
    numerator, denominator = sums(units, lambda k: weights[k], lambda k: scratch[k], 4)
    out_ref[0] = numerator.astype(out_ref.dtype)
    out_ref[1] = denominator.astype(out_ref.dtype)


def set_p(place, squares, projection, moved, parts, dy, dtype):
    tall = 128
    pieces = [piece for group in moved for piece in group]
    return pl.pallas_call(
        lambda *refs: set_p_kernel([len(group) for group in moved], *refs),
        grid_spec=pltpu.PrefetchScalarGridSpec(
            num_scalar_prefetch=1,
            grid=(UNITS // tall,),
            in_specs=[
                pl.BlockSpec((tall, TOK), lambda u, s: (u, 0)),
                pl.BlockSpec((tall, WIDE), lambda u, s: (u, lax.rem(s[0] + dy, 2) * 4 + s[1])),
            ]
            + [pl.BlockSpec((tall, width), lambda u, s, i=i: (u, i)) for _, width, i in pieces]
            + [pl.BlockSpec((4, 4, 64, WP), lambda u, s: (0, 0, 0, dy))] * 2,
            out_specs=pl.BlockSpec((2, tall, WP), lambda u, s: (0, u, 0)),
            scratch_shapes=[pltpu.VMEM((4, TOK, WP), BF)],
        ),
        out_shape=shape(2, UNITS, WP, dtype=dtype),
        compiler_params=pltpu.CompilerParams(vmem_limit_bytes=VMEM),
        cost_estimate=SMALL,
    )(place, squares, projection, *[array for array, _, _ in pieces], *parts)


def set_q_kernel(place_ref, own_units, far_units, own_0, own_1, own_2, own_3, far_weights, *refs):
    own_weights = (own_0, own_1, own_2, own_3)
    parts, outs, scratch = refs[:2], refs[2:6], refs[6]

    @pl.when(pl.program_id(0) == 0)
    def _():
        place_tokens(parts, scratch)

    for dz in (1, 2, 3, 0):
        columns = slice(dz * WQ, dz * WQ + WQ)
        weights = (own_weights[dz][...], far_weights[:, columns])
        numerator, denominator = sums(
            [own_units[...], far_units[...]], lambda k: weights[k], lambda k: scratch[k, :, columns], 2
        )
        outs[dz][0] = numerator.astype(outs[dz].dtype)
        outs[dz][1] = denominator.astype(outs[dz].dtype)


def set_q(place, units, far_units, projection, far, parts):
    tall = 128

    def own(dz):
        return pl.BlockSpec((tall, WQ), lambda u, s: (u, (s[0] * 4 + lax.rem(s[1] + dz, 4)) * (WIDE // WQ) + WP // WQ))

    return pl.pallas_call(
        set_q_kernel,
        grid_spec=pltpu.PrefetchScalarGridSpec(
            num_scalar_prefetch=1,
            grid=(UNITS // tall,),
            in_specs=[
                pl.BlockSpec((tall, TOK), lambda u, s: (u, 0)),
                pl.BlockSpec((tall, TOK), lambda u, s: (u, 0)),
            ]
            + [own(dz) for dz in range(4)]
            + [pl.BlockSpec((tall, 4 * WQ), lambda u, s: (u, 0))]
            + [pl.BlockSpec((4, 2, 64, 4 * WQ), lambda u, s: (0, 0, 0, 0))] * 2,
            out_specs=[pl.BlockSpec((2, tall, WQ), lambda u, s: (0, u, 0))] * 4,
            scratch_shapes=[pltpu.VMEM((2, TOK, 4 * WQ), BF)],
        ),
        out_shape=[shape(2, UNITS, WQ)] * 4,
        compiler_params=pltpu.CompilerParams(vmem_limit_bytes=VMEM),
        cost_estimate=SMALL,
    )(place, units, far_units, projection, projection, projection, projection, far, *parts)


def quotient_kernel(n_given, *refs):
    out_ref = refs[-1]

    def total(i):
        value = refs[0][i].astype(F32)
        for ref in refs[1 : -1 - n_given]:
            value = value + ref[i].astype(F32)
        return value

    out_ref[...] = total(0) / (total(1) + TOK * 1e-06)


def quotient(columns, terms, before=None, tall=224):
    width = columns.stop - columns.start
    place = columns.start // width
    given = [] if before is None else [before]
    return pl.pallas_call(
        lambda *refs: quotient_kernel(len(given), *refs),
        grid=(UNITS // tall,),
        in_specs=[pl.BlockSpec((2, tall, width), lambda u: (0, u, 0))] * len(terms)
        + [pl.BlockSpec(memory_space=pl.ANY)] * len(given),
        out_specs=pl.BlockSpec((tall, width), lambda u: (u, place)),
        out_shape=shape(UNITS, WIDE, dtype=F32),
        input_output_aliases={len(terms): 0} if given else {},
        compiler_params=pltpu.CompilerParams(vmem_limit_bytes=VMEM),
        cost_estimate=SMALL,
    )(*terms, *given)


def body(token_rows, gate_cache, up_cache, down_weight, targets):
    y, z, x, core = (lax.axis_index(name) for name in ("y_lo", "z", "x", "core"))
    place = jnp.stack([y, z, x, core]).astype(jnp.int32)
    projection = down_weight[0]

    def send(value, axis, k=1):
        return lax.ppermute(value, axis, shift(k) if axis in ("z", "x") else SWAP)

    together = lax.optimization_barrier

    hidden, squares = make_hidden(place, token_rows, gate_cache[0], up_cache[0])

    own_p, other_p = partial_outputs(hidden, projection, 0, WP)
    other_p, squares = together((other_p, squares))
    side, one, three = cut(
        cut_first_kernel, place, [squares], projection,
        [(0, 1), (0, 3), (1, 0), (1, 1), (1, 2), (1, 3)], [4 * WQ, WP + WN + TOK, WP + WN + TOK],
    )
    one, three, side = send(one, "z", 1), send(three, "z", 3), send(side, "y_lo")

    def pair(own, other):
        both = (own.astype(F32) + send(other, "core").astype(F32)).astype(BF)
        return both.reshape(4, 64, -1)

    def over_x(blocks):
        return lax.all_to_all(blocks, "x", 0, 0, tiled=True)

    def total(blocks):
        return jnp.sum(blocks.astype(F32), axis=0).astype(BF)

    def four(part):
        return jnp.broadcast_to(part[None], (4,) + part.shape)

    pair_p, hidden = together((pair(own_p, other_p), hidden))
    blocks_p = over_x(pair_p)
    pair_q = pair(*partial_outputs(hidden, projection, WP, WIDE))
    blocks_p, pair_q = together((blocks_p, pair_q))
    total_p = total(blocks_p)
    total_p, side = together((total_p, side))
    far_p = send(total_p, "y_hi")
    blocks_q = over_x(pair_q)
    squares_p = error_squares(
        place, total_p, far_p, targets[0], 0, WP, [shape(64, 2 * WP)] * 4,
        [pl.BlockSpec((64, WP), lambda j, s: (0, lax.rem(j + s[0], 2)))] * 4, put_p,
    )
    late_1, early_2, late_2, late_3, far_2 = cut(
        cut_second_kernel, place, [], projection,
        [(0, 1), (0, 2), (0, 3), (1, 2)], [WP - WN, WN2, WP - WN2, WP - WN, WP],
    )
    squares_p, one, three, blocks_q, far_2, early_2, late = together(
        (squares_p, one, three, blocks_q, far_2, early_2, (late_1, late_2, late_3))
    )
    total_q = total(blocks_q)
    far_q = send(total_q, "y_hi")
    mine_p = jnp.stack([squares_p[0]] + [send(squares_p[k], "z", k) for k in (1, 2, 3)])
    middle = WP + TOK // 2
    u_2 = (one[:, WP:middle], three[:, middle : WP + TOK])
    mine_p, far_2, u_2, squares_late = together((mine_p, far_2, u_2, squares))

    u_2 = (send(u_2[0], "z", 1), send(u_2[1], "z", 3))
    far_2, u_side = send(far_2, "z", 2), send(squares_late, "y_lo")
    row_p = over_x(four(mine_p))
    squares_q = error_squares(
        place, total_q, far_q, targets[0], WP, WIDE, shape(2, 64, 4 * WQ),
        pl.BlockSpec((1, 64, 4 * WQ), lambda j, s: (lax.rem(j + s[0], 2), 0, 0)), put_q,
    )
    mine_q = jnp.stack([squares_q[0], send(squares_q[1], "y_lo")])
    row_p, far_2, u_2, u_side, mine_q, early_2, late = together(
        (row_p, far_2, u_2, u_side, mine_q, early_2, late)
    )

    half = TOK // 2

    def units_in(array):
        return [(array, half, WP // half), (array, half, WP // half + 1)]

    def near_in(array, late):
        return [(array, WN, (WP + TOK) // WN), (late, WP - WN, 0)]

    units = [units_in(one), [(u, half, 0) for u in u_2], units_in(three)]
    fars = [[(array, WP, 0)] for array in (one, far_2, three)]
    early_2 = send(early_2, "z", 2)
    parts_p = [row_p, send(row_p, "core")]
    p_far = send(set_p(place, squares, projection, units + fars, parts_p, 1, BF), "y_lo")
    row_q, early_2, late = together((over_x(four(mine_q)), early_2, late))
    late = [send(piece, "z", k + 1) for k, piece in enumerate(late)]
    parts_q = [row_q, send(row_q, "core")]
    q_sums = set_q(place, squares, u_side, projection, side, parts_q)
    q_own, *q_send = q_sums
    q_send[1], late = together((q_send[1], late))
    q_far = [send(q, "z", k + 1) for k, q in enumerate(q_send)]
    nears = [
        near_in(one, late[0]),
        [(early_2, WN2, 0), (late[1], WP - WN2, 0)],
        near_in(three, late[2]),
    ]
    p_own = set_p(place, squares, projection, units + nears, parts_p, 0, BF)
    merged = quotient(slice(0, WP), [p_own, p_far])
    return quotient(slice(WP, WIDE), [q_own, *q_far], merged, 448)


def solution(mesh):
    cut = Mesh(mesh.devices.reshape(2, 4, 2, 4, 2), ("y_lo", "z", "y_hi", "x", "core"))
    ft, tp = ("y_lo", "z"), ("y_hi", "x", "core")
    placed = (P(ft, None), P(ft, None, tp), P(ft, None, tp), P(ft, tp, None), P(ft, None, None))
    return jax.shard_map(body, mesh=cut, in_specs=placed, out_specs=P(tp, ft), check_vma=False)
```
